256 devices in a mesh: loop: 64 (over x, y_hi, z), grp: 4 (over y_lo, core).
Axes of the slice: x: 4, y: 4 (y_hi: 2, y_lo: 2; y = y_hi * 2 + y_lo), z: 8, core: 2. Of those that a mesh axis runs over, the one named last changes fastest.
Arguments:
- student_image: bfloat16 [98304, 768], P(('loop', 'grp')), may hold values from -64 to 64
- student_text: bfloat16 [98304, 768], P(('loop', 'grp')), may hold values from -64 to 64
- teacher_image: bfloat16 [98304, 1152], P(('loop', 'grp')), may hold values from -64 to 64
- teacher_text: bfloat16 [98304, 1152], P(('loop', 'grp')), may hold values from -64 to 64
- student_scale: float32 [1], replicated, may hold values from 10 to 40
- student_bias: float32 [1], replicated, may hold values from -3 to 1
- teacher_scale: float32 [1], replicated, may hold values from 50 to 150
- teacher_bias: float32 [1], replicated, may hold values from -4 to 0
Outputs:
- grad_image: float32 [98304, 768], P(('loop', 'grp'))
- grad_text: float32 [98304, 768], P(('loop', 'grp'))
The draws below stay inside these ranges and needn't reach their ends.
All inputs are finite; a program needn't handle non-finite values.
Results may differ from the reference program's by a relative error of at most 0.0065.
Values may be sent and summed in bfloat16 or wider, within the bound.
A program may use at most 64 MiB of HBM per device.

```python
import math
import jax
import jax.numpy as jnp
from jax import lax

D_S = 768
D_T = 1152
TOK_DEV = 384
STEPS = 2
TOKENS = 98304
N_LOOP = 64
N_GRP = 4


def embed_rows(key, width, top_scale):
    keys = jax.random.split(key, 4)
    gaussian = jax.random.truncated_normal(keys[0], -5.0, 5.0, (TOKENS, width), jnp.float32)
    row_scale = jnp.exp(jax.random.uniform(keys[3], (TOKENS, 1), jnp.float32, 0.0, 1.0) * jnp.log(top_scale))
    return (gaussian * row_scale).astype(jnp.bfloat16)


def draw_student_image(key, part):
    key = jax.random.fold_in(key, 21)
    return embed_rows(key, D_S, 10.0)


def draw_student_text(key, part):
    key = jax.random.fold_in(key, 22)
    return embed_rows(key, D_S, 10.0)


def draw_teacher_image(key, part):
    key = jax.random.fold_in(key, 23)
    return embed_rows(key, D_T, 10.0)


def draw_teacher_text(key, part):
    key = jax.random.fold_in(key, 24)
    return embed_rows(key, D_T, 10.0)


def setup_inputs(seed: int = 0) -> dict:
    splits = jax.random.split(jax.random.key(seed), 9)
    student_image = draw_student_image(jax.random.fold_in(splits[8], 71), 0)
    student_text = draw_student_text(jax.random.fold_in(splits[8], 71), 0)
    teacher_image = draw_teacher_image(jax.random.fold_in(splits[8], 71), 0)
    teacher_text = draw_teacher_text(jax.random.fold_in(splits[8], 71), 0)
    student_scale = jnp.clip(jnp.exp(jax.random.uniform(splits[4], (1,), jnp.float32, math.log(10.0), math.log(40.0))), 10.0, 40.0)
    student_bias = jnp.clip(jax.random.uniform(splits[5], (1,), jnp.float32, -3.0, 1.0), -3.0, 1.0)
    teacher_scale = jnp.clip(jnp.exp(jax.random.uniform(splits[6], (1,), jnp.float32, math.log(50.0), math.log(150.0))), 50.0, 150.0)
    teacher_bias = jnp.clip(jax.random.uniform(splits[7], (1,), jnp.float32, -4.0, 0.0), -4.0, 0.0)
    return {"student_image": student_image, "student_text": student_text, "teacher_image": teacher_image, "teacher_text": teacher_text, "student_scale": student_scale, "student_bias": student_bias, "teacher_scale": teacher_scale, "teacher_bias": teacher_bias}


def unit_rows(values):
    wide = values.astype(jnp.float32)
    inverse = lax.rsqrt(lax.optimization_barrier(jnp.sum(wide * wide, axis=-1, keepdims=True)) + 1e-06)
    return (wide * inverse, inverse)

def pair_terms(image_half, teach_image, text_half, teach_text, student_scale, student_bias, teacher_scale, teacher_bias):
    teach = jnp.dot(teach_image, teach_text.T, preferred_element_type=jnp.float32)
    target = jax.nn.sigmoid(teacher_scale * teach + teacher_bias)
    logits = student_scale * jnp.dot(image_half, text_half.T, preferred_element_type=jnp.float32) + student_bias
    weight = (jax.nn.sigmoid(logits) - target).astype(jnp.bfloat16)
    image_pull = jnp.dot(weight, text_half, preferred_element_type=jnp.float32)
    text_pull = jnp.dot(weight.T, image_half, preferred_element_type=jnp.float32)
    return (image_pull, text_pull)

def project_out(pull, unit, inverse, scale):
    grown = scale * pull
    return (grown - unit * lax.optimization_barrier(jnp.sum(unit * grown, axis=-1, keepdims=True))) * inverse

def reference(student_image, student_text, teacher_image, teacher_text, student_scale, student_bias, teacher_scale, teacher_bias):
    width = TOK_DEV * N_GRP
    image_unit, image_inv = unit_rows(student_image)
    text_unit, text_inv = unit_rows(student_text)
    image_half = image_unit.astype(jnp.bfloat16).reshape(N_LOOP, width, D_S)
    text_half = text_unit.astype(jnp.bfloat16).reshape(N_LOOP, width, D_S)
    teach_image = unit_rows(teacher_image)[0].astype(jnp.bfloat16).reshape(N_LOOP, width, D_T)
    teach_text = unit_rows(teacher_text)[0].astype(jnp.bfloat16).reshape(N_LOOP, width, D_T)

    def visit(text_total, index):
        image_total = jnp.zeros((width, D_S), jnp.float32)
        for offset in range(STEPS):
            source = ((index - offset) % N_LOOP).astype(jnp.int32)
            image_pull, text_pull = pair_terms(image_half[index], teach_image[index], text_half[source], teach_text[source], student_scale, student_bias, teacher_scale, teacher_bias)
            image_total = image_total + image_pull
            text_total = text_total.at[source].add(text_pull)
        return (text_total, image_total)
    start = jnp.zeros((N_LOOP, width, D_S), jnp.float32)
    text_total, image_total = lax.scan(visit, start, jnp.arange(N_LOOP, dtype=jnp.int32))
    image_total = image_total.reshape(TOKENS, D_S)
    text_total = text_total.reshape(TOKENS, D_S)
    grad_image = project_out(image_total, image_unit, image_inv, student_scale)
    grad_text = project_out(text_total, text_unit, text_inv, student_scale)
    return (grad_image, grad_text)
```

```python
import functools

import jax
import jax.numpy as jnp
from jax import lax
from jax.experimental import pallas as pl
from jax.experimental.pallas import tpu as pltpu
from jax.sharding import PartitionSpec as P

MESH = pl.DeviceIdType.MESH
N_LOOP = 64
RUN = 8
ROWS = 384
D_S = 768
D_T = 1152
CHUNKS = ((0, 128), (128, 128), (256, 64), (320, 64))
N_CH = len(CHUNKS)
PULL = 64
N_PULL = ROWS // PULL
OWN_TEXT = 2 * ROWS

NT = (((1,), (1,)), ((), ()))
TN = (((0,), (0,)), ((), ()))


def partners():
    loop = lax.axis_index("loop")
    grp = lax.axis_index("grp")
    chip = grp // 2
    core = grp % 2
    seam_next = ((loop % RUN) + 1) // RUN
    seam_prev = (((N_LOOP - loop) % RUN) + RUN - 1) // RUN
    seam_prev = 1 - seam_prev
    across = (loop, (1 - chip) * 2 + core)
    sibling = (loop, chip * 2 + 1 - core)
    after = ((loop + 1) % N_LOOP, ((chip + seam_next) % 2) * 2 + core)
    before = ((loop + N_LOOP - 1) % N_LOOP, ((chip + seam_prev) % 2) * 2 + core)
    return across, sibling, after, before


def kernel(
    ss_ref, sb_ref, ts_ref, tb_ref, si_hbm, st_hbm, ti_hbm, tt_hbm, gi_hbm, gt_hbm,
    raw_si, raw_st, raw_ti, raw_tt, inv_i, inv_t,
    SI, TI, ST, TT, TG, W,
    img_own, txt_own, prev_own,
    y_out, y_in, dt_out, dt_in, dp_out, dp_in, z_out, z_in,
    gi_buf, gt_buf,
    in_sem, out_sem,
    y_s, y_r, z_s, z_r, d_s, d_r, f_s, f_r,
    yp_s, yp_r, dt_s, dt_r, dp_s, dp_r, zp_s, zp_r,
):
    across, sibling, after, before = partners()
    s_scale, s_bias, t_scale, t_bias = ss_ref[0], sb_ref[0], ts_ref[0], tb_ref[0]

    def remote(src, dst, ssem, rsem, dev):
        return pltpu.make_async_remote_copy(
            src_ref=src, dst_ref=dst, send_sem=ssem, recv_sem=rsem,
            device_id=dev, device_id_type=MESH,
        )

    loads = []
    for k, (r, m) in enumerate(CHUNKS):
        rows = pl.ds(r, m)
        loads.append([
            pltpu.make_async_copy(src.at[rows], dst.at[rows], in_sem.at[k, n])
            for n, (src, dst) in enumerate(
                ((ti_hbm, raw_ti), (si_hbm, raw_si), (tt_hbm, raw_tt), (st_hbm, raw_st))
            )
        ])
    for group in loads:
        for copy in group:
            copy.start()
    barrier = pltpu.get_barrier_semaphore()
    for dev in (across, sibling, after, before):
        pl.semaphore_signal(barrier, inc=1, device_id=dev, device_id_type=MESH)

    def unit(raw, rows, out, at, keep=None):
        wide = raw[rows].astype(jnp.float32)
        inverse = lax.rsqrt(jnp.sum(wide * wide, axis=-1, keepdims=True) + 1e-06)
        out[at] = (wide * inverse).astype(jnp.bfloat16)
        if keep is not None:
            keep[rows] = inverse

    def prev_at(k):
        r, m = CHUNKS[k]
        return pl.ds(OWN_TEXT + 2 * r, m), pl.ds(OWN_TEXT + 2 * r + m, m)

    y_cp, z_cp, d_cp, f_cp = [], [], [], []
    for k, (r, m) in enumerate(CHUNKS):
        own = pl.ds(r, m)
        po, ps = prev_at(k)
        y_cp.append((
            remote(TI.at[own], TI.at[pl.ds(ROWS + r, m)], y_s.at[2 * k], y_r.at[2 * k], across),
            remote(SI.at[own], SI.at[pl.ds(ROWS + r, m)], y_s.at[2 * k + 1], y_r.at[2 * k + 1], across),
        ))
        z_cp.append((
            remote(TT.at[own], TT.at[po], z_s.at[2 * k], z_r.at[2 * k], after),
            remote(ST.at[own], ST.at[po], z_s.at[2 * k + 1], z_r.at[2 * k + 1], after),
        ))
        d_cp.append((
            remote(TT.at[own], TT.at[pl.ds(ROWS + r, m)], d_s.at[2 * k], d_r.at[2 * k], sibling),
            remote(ST.at[own], ST.at[pl.ds(ROWS + r, m)], d_s.at[2 * k + 1], d_r.at[2 * k + 1], sibling),
        ))
        f_cp.append((
            remote(TT.at[po], TT.at[ps], f_s.at[2 * k], f_r.at[2 * k], sibling),
            remote(ST.at[po], ST.at[ps], f_s.at[2 * k + 1], f_r.at[2 * k + 1], sibling),
        ))

    for k, (r, m) in enumerate(CHUNKS):
        own = pl.ds(r, m)
        for copy in loads[k]:
            copy.wait()
        unit(raw_ti, own, TI, own)
        unit(raw_tt, own, TT, own)
        if k == 0:
            pl.semaphore_wait(barrier, 4)
        y_cp[k][0].start()
        z_cp[k][0].start()
        unit(raw_si, own, SI, own, inv_i)
        unit(raw_st, own, ST, own, inv_t)
        y_cp[k][1].start()
        z_cp[k][1].start()
        d_cp[k][0].start()
        d_cp[k][1].start()

    def teach(i, m, j, n):
        dot = lax.dot_general(TI[pl.ds(i, m)], TT[pl.ds(j, n)], NT, preferred_element_type=jnp.float32)
        TG[pl.ds(i, m), pl.ds(j, n)] = jax.nn.sigmoid(t_scale * dot + t_bias)

    def study(i, m, j, n):
        dot = lax.dot_general(SI[pl.ds(i, m)], ST[pl.ds(j, n)], NT, preferred_element_type=jnp.float32)
        at = (pl.ds(i, m), pl.ds(j, n))
        W[at] = (jax.nn.sigmoid(s_scale * dot + s_bias) - TG[at]).astype(jnp.bfloat16)

    teach(0, ROWS, 0, ROWS)
    study(0, ROWS, 0, ROWS)
    for k in range(N_CH):
        for copy in d_cp[k]:
            copy.wait_recv()
    teach(0, ROWS, ROWS, ROWS)
    study(0, ROWS, ROWS, ROWS)

    for k, (r, m) in enumerate(CHUNKS):
        j = OWN_TEXT + 2 * r
        for half, tile in ((0, teach), (1, study)):
            z_cp[k][half].wait_recv()
            f_cp[k][half].start()
            y_cp[k][half].wait_recv()
            tile(ROWS + r, m, 0, j)
            f_cp[k][half].wait_recv()
            tile(0, ROWS + r + m, j, 2 * m)

    yp_cp = [
        remote(y_out.at[pl.ds(c * PULL, PULL)], y_in.at[pl.ds(c * PULL, PULL)], yp_s.at[c], yp_r.at[c], across)
        for c in range(N_PULL)
    ]
    zp_cp = [
        remote(z_out.at[pl.ds(r, m)], z_in.at[pl.ds(r, m)], zp_s.at[k], zp_r.at[k], before)
        for k, (r, m) in enumerate(CHUNKS)
    ]
    dp_cp = [
        remote(dp_out.at[pl.ds(r, m)], dp_in.at[pl.ds(r, m)], dp_s.at[k], dp_r.at[k], sibling)
        for k, (r, m) in enumerate(CHUNKS)
    ]
    dt_cp = remote(dt_out, dt_in, dt_s.at[0], dt_r.at[0], sibling)

    def image_pull(i, m):
        return jnp.dot(W[pl.ds(i, m), :], ST[...], preferred_element_type=jnp.float32)

    def text_pull(j, n):
        return lax.dot_general(W[:, pl.ds(j, n)], SI[...], TN, preferred_element_type=jnp.float32)

    def across_pull(c, n):
        y_out[pl.ds(c * PULL, n * PULL)] = image_pull(ROWS + c * PULL, n * PULL).astype(jnp.bfloat16)
        for i in range(c, c + n):
            yp_cp[i].start()

    def prev_pull(k):
        r, m = CHUNKS[k]
        pull = text_pull(OWN_TEXT + 2 * r, 2 * m)
        prev_own[pl.ds(r, m)] = pull[:m]
        dp_out[pl.ds(r, m)] = pull[m:].astype(jnp.bfloat16)
        dp_cp[k].start()

    def prev_send(k):
        r, m = CHUNKS[k]
        rows = pl.ds(r, m)
        dp_cp[k].wait_recv()
        z_out[rows] = (prev_own[rows] + dp_in[rows].astype(jnp.float32)).astype(jnp.bfloat16)
        zp_cp[k].start()

    across_pull(0, 2)
    prev_pull(0)
    across_pull(2, 4)
    prev_pull(1)
    prev_send(0)
    prev_pull(2)
    prev_send(1)
    prev_pull(3)
    prev_send(2)
    prev_send(3)
    dt_out[...] = text_pull(ROWS, ROWS).astype(jnp.bfloat16)
    dt_cp.start()
    img_own[...] = image_pull(0, ROWS)
    txt_own[...] = text_pull(0, ROWS)
    dt_cp.wait_recv()

    def project(pull, raw, inverse, scale):
        row = raw.astype(jnp.float32) * inverse
        grown = scale * pull
        return (grown - row * jnp.sum(row * grown, axis=-1, keepdims=True)) * inverse

    outs = []

    def finish_image(c):
        rows = pl.ds(c * PULL, PULL)
        yp_cp[c].wait_recv()
        pull = img_own[rows] + y_in[rows].astype(jnp.float32)
        gi_buf[rows] = project(pull, raw_si[rows], inv_i[rows], s_scale)
        outs.append(pltpu.make_async_copy(gi_buf.at[rows], gi_hbm.at[rows], out_sem.at[len(outs)]))
        outs[-1].start()

    def finish_text(k):
        r, m = CHUNKS[k]
        rows = pl.ds(r, m)
        zp_cp[k].wait_recv()
        pull = txt_own[rows] + dt_in[rows].astype(jnp.float32) + z_in[rows].astype(jnp.float32)
        gt_buf[rows] = project(pull, raw_st[rows], inv_t[rows], s_scale)
        outs.append(pltpu.make_async_copy(gt_buf.at[rows], gt_hbm.at[rows], out_sem.at[len(outs)]))
        outs[-1].start()

    for step in ((0,), (1,), (2, 0), (3,), (4, 1), (5, 2), (None, 3)):
        if step[0] is not None:
            finish_image(step[0])
        if len(step) > 1:
            finish_text(step[1])

    for group in (*y_cp, *z_cp, *d_cp, *f_cp, yp_cp, zp_cp, dp_cp, (dt_cp,)):
        for copy in group:
            copy.wait_send()
    for copy in outs:
        copy.wait()


def per_device(si, st, ti, tt, ss, sb, ts, tb):
    half, full = jnp.bfloat16, jnp.float32
    dma = pltpu.SemaphoreType.DMA
    smem = pl.BlockSpec(memory_space=pltpu.SMEM)
    hbm = pl.BlockSpec(memory_space=pl.ANY)
    part = lambda dtype: pltpu.VMEM((ROWS, D_S), dtype)
    return pl.pallas_call(
        kernel,
        out_shape=(jax.ShapeDtypeStruct((ROWS, D_S), full),) * 2,
        in_specs=[smem] * 4 + [hbm] * 4,
        out_specs=(hbm, hbm),
        scratch_shapes=[
            part(half), part(half), pltpu.VMEM((ROWS, D_T), half), pltpu.VMEM((ROWS, D_T), half),
            pltpu.VMEM((ROWS, 1), full), pltpu.VMEM((ROWS, 1), full),
            pltpu.VMEM((2 * ROWS, D_S), half), pltpu.VMEM((2 * ROWS, D_T), half),
            pltpu.VMEM((4 * ROWS, D_S), half), pltpu.VMEM((4 * ROWS, D_T), half),
            pltpu.VMEM((2 * ROWS, 4 * ROWS), full), pltpu.VMEM((2 * ROWS, 4 * ROWS), half),
            part(full), part(full), part(full),
            *[part(half)] * 8,
            part(full), part(full),
            dma((N_CH, 4)), dma((N_PULL + N_CH,)),
            *[dma((2 * N_CH,))] * 8,
            dma((N_PULL,)), dma((N_PULL,)), dma((1,)), dma((1,)),
            *[dma((N_CH,))] * 4,
        ],
        compiler_params=pltpu.CompilerParams(
            collective_id=0, has_side_effects=True, vmem_limit_bytes=56 * 2**20,
        ),
    )(ss, sb, ts, tb, si, st, ti, tt)


def solution(mesh):
    row = P(("loop", "grp"), None)
    return jax.shard_map(
        per_device,
        mesh=mesh,
        in_specs=(row, row, row, row, P(), P(), P(), P()),
        out_specs=(row, row),
        check_vma=False,
    )
```

```python
import functools

import jax
import jax.numpy as jnp
from jax import lax
from jax.experimental import pallas as pl
from jax.experimental.pallas import tpu as pltpu
from jax.sharding import PartitionSpec as P

MESH = pl.DeviceIdType.MESH
N_LOOP = 64
HOP = 3
RUN = 2 * HOP + 2
ROWS = 384
D_S = 768
D_T = 1152
CHUNKS = ((0, 128), (128, 128), (256, 64), (320, 64))
N_CH = len(CHUNKS)
FAR = (2, 3)
FAR_ROWS = 128
N_WRITE = 4
PULL = 64
N_PULL = ROWS // PULL
OWN_TEXT = 2 * ROWS

NT = (((1,), (1,)), ((), ()))
TN = (((0,), (0,)), ((), ()))


def partners():
    loop = lax.axis_index("loop")
    grp = lax.axis_index("grp")
    chip = grp // 2
    core = grp % 2
    place = loop % RUN
    swapped = (1 - chip) * 2 + core

    def at(step, swap):
        side = jnp.where(swap, swapped, grp)
        return ((loop + step + N_LOOP) % N_LOOP, side)

    across = (loop, swapped)
    sibling = (loop, chip * 2 + 1 - core)
    after = at(1, place == RUN - 1)
    before = at(-1, place == 0)
    return place, across, sibling, after, before, at


def kernel(
    ss_ref, sb_ref, ts_ref, tb_ref, si_hbm, st_hbm, ti_hbm, tt_hbm, gi_hbm, gt_hbm,
    raw_si, raw_st, raw_ti, raw_tt, inv_i, inv_t,
    SI, TI, ST, TT, TG, W,
    img_own, txt_own, prev_own,
    y_out, y_in, dt_out, dt_in, dp_out, dp_in, z_out, z_in,
    gi_buf, gt_buf,
    far_t, far_s,
    in_sem, out_sem,
    q_s, q_r,
    y_s, y_r, z_s, z_r, d_s, d_r, f_s, f_r,
    yp_s, yp_r, dt_s, dt_r, dp_s, dp_r, zp_s, zp_r,
):
    place, across, sibling, after, before, at = partners()
    s_scale, s_bias, t_scale, t_bias = ss_ref[0], sb_ref[0], ts_ref[0], tb_ref[0]

    def remote(src, dst, ssem, rsem, dev):
        return pltpu.make_async_remote_copy(
            src_ref=src, dst_ref=dst, send_sem=ssem, recv_sem=rsem,
            device_id=dev, device_id_type=MESH,
        )

    loads = []
    for k, (r, m) in enumerate(CHUNKS):
        rows = pl.ds(r, m)
        loads.append([
            pltpu.make_async_copy(src.at[rows], dst.at[rows], in_sem.at[k, n])
            for n, (src, dst) in enumerate(
                ((ti_hbm, raw_ti), (si_hbm, raw_si), (tt_hbm, raw_tt), (st_hbm, raw_st))
            )
        ])
    for group in loads:
        for copy in group:
            copy.start()
    barrier = pltpu.get_barrier_semaphore()
    for dev in (across, sibling, before):
        pl.semaphore_signal(barrier, inc=1, device_id=dev, device_id_type=MESH)
    relays = place % HOP == 1

    @pl.when(place == 1 + HOP)
    def _():
        pl.semaphore_signal(barrier, inc=1, device_id=at(HOP, False), device_id_type=MESH)

    @pl.when(place == 1)
    def _():
        pl.semaphore_signal(barrier, inc=1, device_id=at(HOP - RUN, True), device_id_type=MESH)

    @pl.when(place == 0)
    def _():
        pl.semaphore_signal(barrier, inc=1, device_id=at(1, False), device_id_type=MESH)


    def unit(raw, rows, out, at, keep=None):
        wide = raw[rows].astype(jnp.float32)
        inverse = lax.rsqrt(jnp.sum(wide * wide, axis=-1, keepdims=True) + 1e-06)
        out[at] = (wide * inverse).astype(jnp.bfloat16)
        if keep is not None:
            keep[rows] = inverse

    def prev_at(k):
        r, m = CHUNKS[k]
        return pl.ds(OWN_TEXT + 2 * r, m), pl.ds(OWN_TEXT + 2 * r + m, m)

    y_cp, z_cp, d_cp, f_cp, far_cp = [], [], [], [], []
    for k, (r, m) in enumerate(CHUNKS):
        own = pl.ds(r, m)
        po, ps = prev_at(k)
        y_cp.append((
            remote(TI.at[own], TI.at[pl.ds(ROWS + r, m)], y_s.at[2 * k], y_r.at[2 * k], across),
            remote(SI.at[own], SI.at[pl.ds(ROWS + r, m)], y_s.at[2 * k + 1], y_r.at[2 * k + 1], across),
        ))
        z_cp.append((
            remote(TT.at[own], TT.at[po], z_s.at[2 * k], z_r.at[2 * k], after),
            remote(ST.at[own], ST.at[po], z_s.at[2 * k + 1], z_r.at[2 * k + 1], after),
        ))
        d_cp.append((
            remote(TT.at[own], TT.at[pl.ds(ROWS + r, m)], d_s.at[2 * k], d_r.at[2 * k], sibling),
            remote(ST.at[own], ST.at[pl.ds(ROWS + r, m)], d_s.at[2 * k + 1], d_r.at[2 * k + 1], sibling),
        ))
        f_cp.append((
            remote(TT.at[po], TT.at[ps], f_s.at[2 * k], f_r.at[2 * k], sibling),
            remote(ST.at[po], ST.at[ps], f_s.at[2 * k + 1], f_r.at[2 * k + 1], sibling),
        ))
        if k in FAR:
            down, over, home = at(-HOP, False), at(RUN - HOP, True), at(-1, False)
            stop = pl.ds(r - CHUNKS[FAR[0]][0], m)
            pairs = []
            for half, (text, stay) in enumerate(((TT, far_t), (ST, far_s))):
                n = 2 * (k - FAR[0]) + half
                pairs.append((
                    remote(text.at[own], stay.at[stop], q_s.at[n], q_r.at[n], down),
                    remote(stay.at[stop], stay.at[stop], q_s.at[n], q_r.at[n], over),
                    remote(stay.at[stop], text.at[po], q_s.at[n], z_r.at[2 * k + half], home),
                ))
            far_cp.extend(pairs)

    def pass_on(hop, first, last):
        @pl.when(place == 1 + HOP * (2 - hop))
        def _():
            for n in range(first, last):
                far_cp[n][0].wait_recv()
                far_cp[n][hop].start()

    def prepare_images(k):
        own = pl.ds(*CHUNKS[k])
        unit(raw_ti, own, TI, own)
        y_cp[k][0].start()
        unit(raw_si, own, SI, own, inv_i)
        y_cp[k][1].start()

    def prepare_text(k):
        own = pl.ds(*CHUNKS[k])
        unit(raw_tt, own, TT, own)
        unit(raw_st, own, ST, own, inv_t)

    for copy in loads[0]:
        copy.wait()
    own = pl.ds(*CHUNKS[0])
    unit(raw_ti, own, TI, own)
    unit(raw_tt, own, TT, own)
    pl.semaphore_wait(barrier, jnp.where(relays, 4, 3))
    y_cp[0][0].start()
    z_cp[0][0].start()
    unit(raw_si, own, SI, own, inv_i)
    unit(raw_st, own, ST, own, inv_t)
    y_cp[0][1].start()
    z_cp[0][1].start()
    d_cp[0][0].start()
    d_cp[0][1].start()
    for group in loads[1:]:
        for copy in group:
            copy.wait()
    for k in FAR:
        prepare_text(k)

        @pl.when(place == RUN - 1)
        def _():
            for half in (0, 1):
                far_cp[2 * (k - FAR[0]) + half][0].start()
    for k in range(1, N_CH):
        if k not in FAR:
            prepare_text(k)
            for half in (0, 1):
                z_cp[k][half].start()
        for half in (0, 1):
            d_cp[k][half].start()

    @pl.when(place != RUN - 1)
    def _():
        for k in FAR:
            for half in (0, 1):
                z_cp[k][half].start()

    for k in range(1, N_CH):
        prepare_images(k)

    def teach(i, m, j, n):
        dot = lax.dot_general(TI[pl.ds(i, m)], TT[pl.ds(j, n)], NT, preferred_element_type=jnp.float32)
        TG[pl.ds(i, m), pl.ds(j, n)] = jax.nn.sigmoid(t_scale * dot + t_bias)

    def study(i, m, j, n):
        dot = lax.dot_general(SI[pl.ds(i, m)], ST[pl.ds(j, n)], NT, preferred_element_type=jnp.float32)
        at = (pl.ds(i, m), pl.ds(j, n))
        W[at] = (jax.nn.sigmoid(s_scale * dot + s_bias) - TG[at]).astype(jnp.bfloat16)

    teach(0, ROWS, 0, ROWS)
    study(0, ROWS, 0, ROWS)
    for k in range(N_CH):
        for copy in d_cp[k]:
            copy.wait_recv()
    teach(0, ROWS, ROWS, ROWS)
    study(0, ROWS, ROWS, ROWS)

    pass_on(1, 0, 3)
    for k, (r, m) in enumerate(CHUNKS):
        j = OWN_TEXT + 2 * r
        for half, tile in ((0, teach), (1, study)):
            z_cp[k][half].wait_recv()
            f_cp[k][half].start()
            y_cp[k][half].wait_recv()
            tile(ROWS + r, m, 0, j)
            f_cp[k][half].wait_recv()
            tile(0, ROWS + r + m, j, 2 * m)
        if k == 0:
            pass_on(1, 3, 4)
            pass_on(2, 0, 2)
        if k == 1:
            pass_on(2, 2, 4)

    yp_cp = [
        remote(y_out.at[pl.ds(c * PULL, PULL)], y_in.at[pl.ds(c * PULL, PULL)], yp_s.at[c], yp_r.at[c], across)
        for c in range(N_PULL)
    ]
    zp_cp = [
        remote(z_out.at[pl.ds(r, m)], z_in.at[pl.ds(r, m)], zp_s.at[k], zp_r.at[k], before)
        for k, (r, m) in enumerate(CHUNKS)
    ]
    dp_cp = [
        remote(dp_out.at[pl.ds(r, m)], dp_in.at[pl.ds(r, m)], dp_s.at[k], dp_r.at[k], sibling)
        for k, (r, m) in enumerate(CHUNKS)
    ]
    dt_cp = remote(dt_out, dt_in, dt_s.at[0], dt_r.at[0], sibling)

    def image_pull(i, m):
        return jnp.dot(W[pl.ds(i, m), :], ST[...], preferred_element_type=jnp.float32)

    def text_pull(j, n):
        return lax.dot_general(W[:, pl.ds(j, n)], SI[...], TN, preferred_element_type=jnp.float32)

    def across_pull(c, n):
        y_out[pl.ds(c * PULL, n * PULL)] = image_pull(ROWS + c * PULL, n * PULL).astype(jnp.bfloat16)
        for i in range(c, c + n):
            yp_cp[i].start()

    def prev_pull(k):
        r, m = CHUNKS[k]
        pull = text_pull(OWN_TEXT + 2 * r, 2 * m)
        prev_own[pl.ds(r, m)] = pull[:m]
        dp_out[pl.ds(r, m)] = pull[m:].astype(jnp.bfloat16)
        dp_cp[k].start()

    def prev_send(k):
        r, m = CHUNKS[k]
        rows = pl.ds(r, m)
        dp_cp[k].wait_recv()
        z_out[rows] = (prev_own[rows] + dp_in[rows].astype(jnp.float32)).astype(jnp.bfloat16)
        zp_cp[k].start()

    across_pull(0, 2)
    prev_pull(0)
    across_pull(2, 4)
    prev_pull(1)
    prev_send(0)
    prev_pull(2)
    prev_send(1)
    prev_pull(3)
    prev_send(2)
    prev_send(3)
    dt_out[...] = text_pull(ROWS, ROWS).astype(jnp.bfloat16)
    dt_cp.start()
    img_own[...] = image_pull(0, ROWS)
    txt_own[...] = text_pull(0, ROWS)
    dt_cp.wait_recv()

    def project(pull, raw, inverse, scale):
        row = raw.astype(jnp.float32) * inverse
        grown = scale * pull
        return (grown - row * jnp.sum(row * grown, axis=-1, keepdims=True)) * inverse

    outs = []

    def finish_image(c):
        rows = pl.ds(c * PULL, PULL)
        yp_cp[c].wait_recv()
        pull = img_own[rows] + y_in[rows].astype(jnp.float32)
        gi_buf[rows] = project(pull, raw_si[rows], inv_i[rows], s_scale)
        outs.append(pltpu.make_async_copy(gi_buf.at[rows], gi_hbm.at[rows], out_sem.at[len(outs)]))
        outs[-1].start()

    def finish_text(k):
        r, m = CHUNKS[k]
        rows = pl.ds(r, m)
        zp_cp[k].wait_recv()
        pull = txt_own[rows] + dt_in[rows].astype(jnp.float32) + z_in[rows].astype(jnp.float32)
        gt_buf[rows] = project(pull, raw_st[rows], inv_t[rows], s_scale)
        outs.append(pltpu.make_async_copy(gt_buf.at[rows], gt_hbm.at[rows], out_sem.at[len(outs)]))
        outs[-1].start()

    for step in ((0,), (1,), (2, 0), (3,), (4, 1), (5, 2), (None, 3)):
        if step[0] is not None:
            finish_image(step[0])
        if len(step) > 1:
            finish_text(step[1])

    for n, copies in enumerate(far_cp):
        @pl.when(relays)
        def _():
            copies[0].wait_send()

        @pl.when(place != RUN - 1)
        def _():
            z_cp[FAR[n // 2]][n % 2].wait_send()

    near = [z_cp[k] for k in range(N_CH) if k not in FAR]
    for group in (*y_cp, *near, *d_cp, *f_cp, yp_cp, zp_cp, dp_cp, (dt_cp,)):
        for copy in group:
            copy.wait_send()
    for copy in outs:
        copy.wait()


def write_kernel(gi_hbm, gt_hbm, gi_out, gt_out, gi_buf, gt_buf, in_sem, out_sem):
    reads, writes = [], []
    for k in range(N_WRITE):
        rows = pl.ds(k * (ROWS // N_WRITE), ROWS // N_WRITE)
        for n, (src, buf, dst) in enumerate(((gi_hbm, gi_buf, gi_out), (gt_hbm, gt_buf, gt_out))):
            reads.append(pltpu.make_async_copy(src.at[rows], buf.at[rows], in_sem.at[k, n]))
            writes.append(pltpu.make_async_copy(buf.at[rows], dst.at[rows], out_sem.at[k, n]))
    for copy in reads:
        copy.start()
    for read, write in zip(reads, writes):
        read.wait()
        write.start()
    for copy in writes:
        copy.wait()


def per_device(si, st, ti, tt, ss, sb, ts, tb):
    half, full = jnp.bfloat16, jnp.float32
    dma = pltpu.SemaphoreType.DMA
    smem = pl.BlockSpec(memory_space=pltpu.SMEM)
    hbm = pl.BlockSpec(memory_space=pltpu.HBM)
    part = lambda dtype: pltpu.VMEM((ROWS, D_S), dtype)
    grads = pl.pallas_call(
        kernel,
        out_shape=(jax.ShapeDtypeStruct((ROWS, D_S), full),) * 2,
        in_specs=[smem] * 4 + [hbm] * 4,
        out_specs=(hbm, hbm),
        scratch_shapes=[
            part(half), part(half), pltpu.VMEM((ROWS, D_T), half), pltpu.VMEM((ROWS, D_T), half),
            pltpu.VMEM((ROWS, 1), full), pltpu.VMEM((ROWS, 1), full),
            pltpu.VMEM((2 * ROWS, D_S), half), pltpu.VMEM((2 * ROWS, D_T), half),
            pltpu.VMEM((4 * ROWS, D_S), half), pltpu.VMEM((4 * ROWS, D_T), half),
            pltpu.VMEM((2 * ROWS, 4 * ROWS), full), pltpu.VMEM((2 * ROWS, 4 * ROWS), half),
            part(full), part(full), part(full),
            *[part(half)] * 8,
            part(full), part(full),
            pltpu.VMEM((FAR_ROWS, D_T), half), pltpu.VMEM((FAR_ROWS, D_S), half),
            dma((N_CH, 4)), dma((N_PULL + N_CH,)),
            dma((2 * len(FAR),)), dma((2 * len(FAR),)),
            *[dma((2 * N_CH,))] * 8,
            dma((N_PULL,)), dma((N_PULL,)), dma((1,)), dma((1,)),
            *[dma((N_CH,))] * 4,
        ],
        compiler_params=pltpu.CompilerParams(
            collective_id=0, has_side_effects=True, vmem_limit_bytes=56 * 2**20,
        ),
    )(ss, sb, ts, tb, si, st, ti, tt)
    return pl.pallas_call(
        write_kernel,
        out_shape=(jax.ShapeDtypeStruct((ROWS, D_S), full),) * 2,
        in_specs=[hbm, hbm],
        out_specs=(hbm, hbm),
        scratch_shapes=[part(full), part(full), dma((N_WRITE, 2)), dma((N_WRITE, 2))],
        compiler_params=pltpu.CompilerParams(vmem_limit_bytes=56 * 2**20),
    )(*grads)


def solution(mesh):
    row = P(("loop", "grp"), None)
    return jax.shard_map(
        per_device,
        mesh=mesh,
        in_specs=(row, row, row, row, P(), P(), P(), P()),
        out_specs=(row, row),
        check_vma=False,
    )
```

```python
import functools

import jax
import jax.numpy as jnp
from jax import lax
from jax.experimental import pallas as pl
from jax.experimental.pallas import tpu as pltpu
from jax.sharding import PartitionSpec as P

MESH = pl.DeviceIdType.MESH
N_LOOP = 64
HOP = 3
RUN = 2 * HOP + 2
ROWS = 384
D_S = 768
D_T = 1152
CHUNKS = ((0, 64), (64, 128), (192, 64), (256, 64), (320, 64))
N_CH = len(CHUNKS)
FAR = (3, 4)
FAR_ROWS = 128
SPLIT = 2
RELAY = ((1, 1, 1, 4), (1, 2, 0, 1), (2, 2, 1, 2), (3, 2, 2, 4))
N_WRITE = 4
PULL = 64
N_PULL = ROWS // PULL
OWN_TEXT = 2 * ROWS

NT = (((1,), (1,)), ((), ()))
TN = (((0,), (0,)), ((), ()))


def partners():
    loop = lax.axis_index("loop")
    grp = lax.axis_index("grp")
    chip = grp // 2
    core = grp % 2
    place = loop % RUN
    swapped = (1 - chip) * 2 + core

    def at(step, swap):
        side = jnp.where(swap, swapped, grp)
        return ((loop + step + N_LOOP) % N_LOOP, side)

    across = (loop, swapped)
    sibling = (loop, chip * 2 + 1 - core)
    after = at(1, place == RUN - 1)
    before = at(-1, place == 0)
    return place, across, sibling, after, before, at


def kernel(
    ss_ref, sb_ref, ts_ref, tb_ref, si_hbm, st_hbm, ti_hbm, tt_hbm, gi_hbm, gt_hbm,
    raw_si, raw_st, raw_ti, raw_tt, inv_i, inv_t,
    SI, TI, ST, TT, TG, W,
    img_own, txt_own, prev_own,
    y_out, y_in, dt_out, dt_in, dp_out, dp_in, z_out, z_in,
    gi_buf, gt_buf,
    far_t, far_s,
    in_sem, out_sem,
    q_s, q_r,
    y_s, y_r, z_s, z_r, d_s, d_r, f_s, f_r,
    yp_s, yp_r, dt_s, dt_r, dp_s, dp_r, zp_s, zp_r,
):
    place, across, sibling, after, before, at = partners()
    s_scale, s_bias, t_scale, t_bias = ss_ref[0], sb_ref[0], ts_ref[0], tb_ref[0]

    def remote(src, dst, ssem, rsem, dev):
        return pltpu.make_async_remote_copy(
            src_ref=src, dst_ref=dst, send_sem=ssem, recv_sem=rsem,
            device_id=dev, device_id_type=MESH,
        )

    loads = []
    for k, (r, m) in enumerate(CHUNKS):
        rows = pl.ds(r, m)
        loads.append([
            pltpu.make_async_copy(src.at[rows], dst.at[rows], in_sem.at[k, n])
            for n, (src, dst) in enumerate(
                ((ti_hbm, raw_ti), (si_hbm, raw_si), (tt_hbm, raw_tt), (st_hbm, raw_st))
            )
        ])
    for group in loads:
        for copy in group:
            copy.start()
    barrier = pltpu.get_barrier_semaphore()
    for dev in (across, sibling, before):
        pl.semaphore_signal(barrier, inc=1, device_id=dev, device_id_type=MESH)
    relays = place % HOP == 1

    @pl.when(place == 1 + HOP)
    def _():
        pl.semaphore_signal(barrier, inc=1, device_id=at(HOP, False), device_id_type=MESH)

    @pl.when(place == 1)
    def _():
        pl.semaphore_signal(barrier, inc=1, device_id=at(HOP - RUN, True), device_id_type=MESH)

    @pl.when(place == 0)
    def _():
        pl.semaphore_signal(barrier, inc=1, device_id=at(1, False), device_id_type=MESH)


    def unit(raw, rows, out, at, keep=None):
        wide = raw[rows].astype(jnp.float32)
        inverse = lax.rsqrt(jnp.sum(wide * wide, axis=-1, keepdims=True) + 1e-06)
        out[at] = (wide * inverse).astype(jnp.bfloat16)
        if keep is not None:
            keep[rows] = inverse

    def prev_at(k):
        r, m = CHUNKS[k]
        return pl.ds(OWN_TEXT + 2 * r, m), pl.ds(OWN_TEXT + 2 * r + m, m)

    y_cp, z_cp, d_cp, f_cp, far_cp = [], [], [], [], []
    for k, (r, m) in enumerate(CHUNKS):
        own = pl.ds(r, m)
        po, ps = prev_at(k)
        y_cp.append((
            remote(TI.at[own], TI.at[pl.ds(ROWS + r, m)], y_s.at[2 * k], y_r.at[2 * k], across),
            remote(SI.at[own], SI.at[pl.ds(ROWS + r, m)], y_s.at[2 * k + 1], y_r.at[2 * k + 1], across),
        ))
        z_cp.append((
            remote(TT.at[own], TT.at[po], z_s.at[2 * k], z_r.at[2 * k], after),
            remote(ST.at[own], ST.at[po], z_s.at[2 * k + 1], z_r.at[2 * k + 1], after),
        ))
        d_cp.append((
            remote(TT.at[own], TT.at[pl.ds(ROWS + r, m)], d_s.at[2 * k], d_r.at[2 * k], sibling),
            remote(ST.at[own], ST.at[pl.ds(ROWS + r, m)], d_s.at[2 * k + 1], d_r.at[2 * k + 1], sibling),
        ))
        f_cp.append((
            remote(TT.at[po], TT.at[ps], f_s.at[2 * k], f_r.at[2 * k], sibling),
            remote(ST.at[po], ST.at[ps], f_s.at[2 * k + 1], f_r.at[2 * k + 1], sibling),
        ))
        if k in FAR:
            down, over, home = at(-HOP, False), at(RUN - HOP, True), at(-1, False)
            stop = pl.ds(r - CHUNKS[FAR[0]][0], m)
            pairs = []
            for half, (text, stay) in enumerate(((TT, far_t), (ST, far_s))):
                n = 2 * (k - FAR[0]) + half
                pairs.append((
                    remote(text.at[own], stay.at[stop], q_s.at[n], q_r.at[n], down),
                    remote(stay.at[stop], stay.at[stop], q_s.at[n], q_r.at[n], over),
                    remote(stay.at[stop], text.at[po], q_s.at[n], z_r.at[2 * k + half], home),
                ))
            far_cp.extend(pairs)

    def pass_on(hop, first, last):
        @pl.when(place == 1 + HOP * (2 - hop))
        def _():
            for n in range(first, last):
                far_cp[n][0].wait_recv()
                far_cp[n][hop].start()

    def prepare_images(k):
        own = pl.ds(*CHUNKS[k])
        unit(raw_ti, own, TI, own)
        y_cp[k][0].start()
        unit(raw_si, own, SI, own, inv_i)
        y_cp[k][1].start()

    def prepare_text(k):
        own = pl.ds(*CHUNKS[k])
        unit(raw_tt, own, TT, own)
        unit(raw_st, own, ST, own, inv_t)

    for copy in loads[0]:
        copy.wait()
    own = pl.ds(*CHUNKS[0])
    unit(raw_ti, own, TI, own)
    unit(raw_tt, own, TT, own)
    pl.semaphore_wait(barrier, jnp.where(relays, 4, 3))
    y_cp[0][0].start()
    z_cp[0][0].start()
    unit(raw_si, own, SI, own, inv_i)
    unit(raw_st, own, ST, own, inv_t)
    y_cp[0][1].start()
    z_cp[0][1].start()
    d_cp[0][0].start()
    d_cp[0][1].start()
    for group in loads[1:]:
        for copy in group:
            copy.wait()
    for k in FAR:
        own = pl.ds(*CHUNKS[k])
        for half, norm in ((0, (raw_tt, own, TT, own)), (1, (raw_st, own, ST, own, inv_t))):
            unit(*norm)

            @pl.when(place == RUN - 1)
            def _():
                far_cp[2 * (k - FAR[0]) + half][0].start()
    for k in range(1, N_CH):
        if k not in FAR:
            prepare_text(k)
            for half in (0, 1):
                z_cp[k][half].start()
        for half in (0, 1):
            d_cp[k][half].start()

    @pl.when(place != RUN - 1)
    def _():
        for k in FAR:
            for half in (0, 1):
                z_cp[k][half].start()

    for k in range(1, N_CH):
        prepare_images(k)

    def teach(i, m, j, n):
        dot = lax.dot_general(TI[pl.ds(i, m)], TT[pl.ds(j, n)], NT, preferred_element_type=jnp.float32)
        TG[pl.ds(i, m), pl.ds(j, n)] = jax.nn.sigmoid(t_scale * dot + t_bias)

    def study(i, m, j, n):
        dot = lax.dot_general(SI[pl.ds(i, m)], ST[pl.ds(j, n)], NT, preferred_element_type=jnp.float32)
        at = (pl.ds(i, m), pl.ds(j, n))
        W[at] = (jax.nn.sigmoid(s_scale * dot + s_bias) - TG[at]).astype(jnp.bfloat16)

    teach(0, ROWS, 0, ROWS)
    study(0, ROWS, 0, ROWS)
    for k in range(N_CH):
        for copy in d_cp[k]:
            copy.wait_recv()
    teach(0, ROWS, ROWS, ROWS)
    study(0, ROWS, ROWS, ROWS)

    def arrive(k, half):
        z_cp[k][half].wait_recv()
        f_cp[k][half].start()

    def step(k):
        r, m = CHUNKS[k]
        j = OWN_TEXT + 2 * r
        for half, tile in ((0, teach), (1, study)):
            arrive(k, half)
            y_cp[k][half].wait_recv()
            if k == N_CH - 1 and half == 1:
                break
            tile(ROWS + r, m, 0, j)
            f_cp[k][half].wait_recv()
            tile(0, ROWS + r + m, j, 2 * m)
        for when, hop, first, last in RELAY:
            if when == k + 1:
                pass_on(hop, first, last)

    yp_cp = [
        remote(y_out.at[pl.ds(c * PULL, PULL)], y_in.at[pl.ds(c * PULL, PULL)], yp_s.at[c], yp_r.at[c], across)
        for c in range(N_PULL)
    ]
    zp_cp = [
        remote(z_out.at[pl.ds(r, m)], z_in.at[pl.ds(r, m)], zp_s.at[k], zp_r.at[k], before)
        for k, (r, m) in enumerate(CHUNKS)
    ]
    dp_cp = [
        remote(dp_out.at[pl.ds(r, m)], dp_in.at[pl.ds(r, m)], dp_s.at[k], dp_r.at[k], sibling)
        for k, (r, m) in enumerate(CHUNKS)
    ]
    dt_cp = remote(dt_out, dt_in, dt_s.at[0], dt_r.at[0], sibling)

    def image_pull(i, m):
        return jnp.dot(W[pl.ds(i, m), :], ST[...], preferred_element_type=jnp.float32)

    def text_pull(j, n):
        return lax.dot_general(W[:, pl.ds(j, n)], SI[...], TN, preferred_element_type=jnp.float32)

    def across_pull(c, n):
        y_out[pl.ds(c * PULL, n * PULL)] = image_pull(ROWS + c * PULL, n * PULL).astype(jnp.bfloat16)
        for i in range(c, c + n):
            yp_cp[i].start()

    def prev_pull(first, last):
        r, rows = CHUNKS[first][0], sum(m for _, m in CHUNKS[first:last])
        pull = text_pull(OWN_TEXT + 2 * r, 2 * rows)
        for k in range(first, last):
            at, m = CHUNKS[k]
            mine = 2 * (at - r)
            prev_own[pl.ds(at, m)] = pull[mine:mine + m]
            dp_out[pl.ds(at, m)] = pull[mine + m:mine + 2 * m].astype(jnp.bfloat16)
            dp_cp[k].start()

    def prev_send(k):
        r, m = CHUNKS[k]
        rows = pl.ds(r, m)
        dp_cp[k].wait_recv()
        z_out[rows] = (prev_own[rows] + dp_in[rows].astype(jnp.float32)).astype(jnp.bfloat16)
        zp_cp[k].start()

    @pl.when(place != 0)
    def _():
        pass_on(1, 0, 1)
        for k in range(N_CH):
            step(k)
        r, m = CHUNKS[-1]
        j = OWN_TEXT + 2 * r
        study(ROWS + r, m, OWN_TEXT, j - OWN_TEXT)
        prev_pull(0, 1)
        study(ROWS + r, m, 0, OWN_TEXT)
        f_cp[N_CH - 1][1].wait_recv()
        study(0, 2 * ROWS, j, 2 * m)

    @pl.when(place == 0)
    def _():
        last = N_CH - 1
        r, m = CHUNKS[last]
        mid = CHUNKS[SPLIT][0]
        j = OWN_TEXT + 2 * mid
        for k in range(last):
            for half, tile in ((0, teach), (1, study)):
                y_cp[k][half].wait_recv()
                tile(ROWS + CHUNKS[k][0], CHUNKS[k][1], 0, OWN_TEXT)
            if k == 1:
                arrive(0, 0)
                arrive(0, 1)
        for k in (*range(1, SPLIT), *FAR[:-1]):
            arrive(k, 0)
            arrive(k, 1)
        for half, tile in ((0, teach), (1, study)):
            for k in range(SPLIT):
                f_cp[k][half].wait_recv()
            tile(0, ROWS + r, OWN_TEXT, j - OWN_TEXT)
        for half, tile in ((0, teach), (1, study)):
            for k in (*range(SPLIT, FAR[0]), last):
                arrive(k, half)
            y_cp[last][half].wait_recv()
            tile(ROWS + r, m, 0, j)
            for k in range(SPLIT, N_CH):
                f_cp[k][half].wait_recv()
            tile(0, 2 * ROWS, j, 2 * (ROWS - mid))
        prev_pull(0, 1)

    across_pull(0, 2)
    prev_send(0)
    prev_pull(1, 2)
    across_pull(2, 4)
    prev_send(1)
    prev_pull(2, N_CH)
    for k in range(2, N_CH):
        prev_send(k)
    dt_out[...] = text_pull(ROWS, ROWS).astype(jnp.bfloat16)
    dt_cp.start()
    img_own[...] = image_pull(0, ROWS)
    txt_own[...] = text_pull(0, ROWS)
    dt_cp.wait_recv()

    def project(pull, raw, inverse, scale):
        row = raw.astype(jnp.float32) * inverse
        grown = scale * pull
        return (grown - row * jnp.sum(row * grown, axis=-1, keepdims=True)) * inverse

    outs = []

    def finish_image(c):
        rows = pl.ds(c * PULL, PULL)
        yp_cp[c].wait_recv()
        pull = img_own[rows] + y_in[rows].astype(jnp.float32)
        gi_buf[rows] = project(pull, raw_si[rows], inv_i[rows], s_scale)
        outs.append(pltpu.make_async_copy(gi_buf.at[rows], gi_hbm.at[rows], out_sem.at[len(outs)]))
        outs[-1].start()

    def finish_text(k):
        r, m = CHUNKS[k]
        rows = pl.ds(r, m)
        zp_cp[k].wait_recv()
        pull = txt_own[rows] + dt_in[rows].astype(jnp.float32) + z_in[rows].astype(jnp.float32)
        gt_buf[rows] = project(pull, raw_st[rows], inv_t[rows], s_scale)
        outs.append(pltpu.make_async_copy(gt_buf.at[rows], gt_hbm.at[rows], out_sem.at[len(outs)]))
        outs[-1].start()

    for image, text in ((0, 0), (1, None), (2, 1), (3, 2), (4, 3), (5, 4)):
        finish_image(image)
        if text is not None:
            finish_text(text)

    for n, copies in enumerate(far_cp):
        @pl.when(relays)
        def _():
            copies[0].wait_send()

        @pl.when(place != RUN - 1)
        def _():
            z_cp[FAR[n // 2]][n % 2].wait_send()

    near = [z_cp[k] for k in range(N_CH) if k not in FAR]
    for group in (*y_cp, *near, *d_cp, *f_cp, yp_cp, zp_cp, dp_cp, (dt_cp,)):
        for copy in group:
            copy.wait_send()
    for copy in outs:
        copy.wait()


def write_kernel(gi_hbm, gt_hbm, gi_out, gt_out, gi_buf, gt_buf, in_sem, out_sem):
    reads, writes = [], []
    for k in range(N_WRITE):
        rows = pl.ds(k * (ROWS // N_WRITE), ROWS // N_WRITE)
        for n, (src, buf, dst) in enumerate(((gi_hbm, gi_buf, gi_out), (gt_hbm, gt_buf, gt_out))):
            reads.append(pltpu.make_async_copy(src.at[rows], buf.at[rows], in_sem.at[k, n]))
            writes.append(pltpu.make_async_copy(buf.at[rows], dst.at[rows], out_sem.at[k, n]))
    for copy in reads:
        copy.start()
    for read, write in zip(reads, writes):
        read.wait()
        write.start()
    for copy in writes:
        copy.wait()


def per_device(si, st, ti, tt, ss, sb, ts, tb):
    half, full = jnp.bfloat16, jnp.float32
    dma = pltpu.SemaphoreType.DMA
    smem = pl.BlockSpec(memory_space=pltpu.SMEM)
    hbm = pl.BlockSpec(memory_space=pltpu.HBM)
    part = lambda dtype: pltpu.VMEM((ROWS, D_S), dtype)
    grads = pl.pallas_call(
        kernel,
        out_shape=(jax.ShapeDtypeStruct((ROWS, D_S), full),) * 2,
        in_specs=[smem] * 4 + [hbm] * 4,
        out_specs=(hbm, hbm),
        scratch_shapes=[
            part(half), part(half), pltpu.VMEM((ROWS, D_T), half), pltpu.VMEM((ROWS, D_T), half),
            pltpu.VMEM((ROWS, 1), full), pltpu.VMEM((ROWS, 1), full),
            pltpu.VMEM((2 * ROWS, D_S), half), pltpu.VMEM((2 * ROWS, D_T), half),
            pltpu.VMEM((4 * ROWS, D_S), half), pltpu.VMEM((4 * ROWS, D_T), half),
            pltpu.VMEM((2 * ROWS, 4 * ROWS), full), pltpu.VMEM((2 * ROWS, 4 * ROWS), half),
            part(full), part(full), part(full),
            *[part(half)] * 8,
            part(full), part(full),
            pltpu.VMEM((FAR_ROWS, D_T), half), pltpu.VMEM((FAR_ROWS, D_S), half),
            dma((N_CH, 4)), dma((N_PULL + N_CH,)),
            dma((2 * len(FAR),)), dma((2 * len(FAR),)),
            *[dma((2 * N_CH,))] * 8,
            dma((N_PULL,)), dma((N_PULL,)), dma((1,)), dma((1,)),
            *[dma((N_CH,))] * 4,
        ],
        compiler_params=pltpu.CompilerParams(
            collective_id=0, has_side_effects=True, vmem_limit_bytes=56 * 2**20,
        ),
    )(ss, sb, ts, tb, si, st, ti, tt)
    return pl.pallas_call(
        write_kernel,
        out_shape=(jax.ShapeDtypeStruct((ROWS, D_S), full),) * 2,
        in_specs=[hbm, hbm],
        out_specs=(hbm, hbm),
        scratch_shapes=[part(full), part(full), dma((N_WRITE, 2)), dma((N_WRITE, 2))],
        compiler_params=pltpu.CompilerParams(vmem_limit_bytes=56 * 2**20),
    )(*grads)


def solution(mesh):
    row = P(("loop", "grp"), None)
    return jax.shard_map(
        per_device,
        mesh=mesh,
        in_specs=(row, row, row, row, P(), P(), P(), P()),
        out_specs=(row, row),
        check_vma=False,
    )
```

```python
import functools

import jax
import jax.numpy as jnp
from jax import lax
from jax.experimental import pallas as pl
from jax.experimental.pallas import tpu as pltpu
from jax.sharding import PartitionSpec as P

MESH = pl.DeviceIdType.MESH
N_LOOP = 64
HOP = 3
RUN = 2 * HOP + 2
ROWS = 384
D_S = 768
D_T = 1152
CHUNKS = ((0, 64), (64, 128), (192, 64), (256, 64), (320, 64))
N_CH = len(CHUNKS)
FAR = (3, 4)
FAR_ROWS = 128
SPLIT = 2
RELAY = ((1, 1, 1, 4), (1, 2, 0, 1), (2, 2, 1, 2), (3, 2, 2, 4))
N_WRITE = 2
PULL = 64
FIRST = 2 * PULL
N_PULL = ROWS // PULL
OWN_TEXT = 2 * ROWS

NT = (((1,), (1,)), ((), ()))
TN = (((0,), (0,)), ((), ()))


def partners():
    loop = lax.axis_index("loop")
    grp = lax.axis_index("grp")
    chip = grp // 2
    core = grp % 2
    place = loop % RUN
    swapped = (1 - chip) * 2 + core

    def at(step, swap):
        side = jnp.where(swap, swapped, grp)
        return ((loop + step + N_LOOP) % N_LOOP, side)

    across = (loop, swapped)
    sibling = (loop, chip * 2 + 1 - core)
    after = at(1, place == RUN - 1)
    before = at(-1, place == 0)
    return place, across, sibling, after, before, at


def kernel(
    ss_ref, sb_ref, ts_ref, tb_ref, si_hbm, st_hbm, ti_hbm, tt_hbm, gi_ref, gt_ref,
    raw_si, raw_st, raw_ti, raw_tt, inv_i, inv_t,
    SI, TI, ST, TT, TG, W,
    img_own, txt_own, prev_own,
    y_out, y_in, dt_out, dt_in, dp_out, dp_in, z_out, z_in,
    far_t, far_s,
    in_sem,
    q_s, q_r,
    y_s, y_r, z_s, z_r, d_s, d_r, f_s, f_r,
    yp_s, yp_r, dt_s, dt_r, dp_s, dp_r, zp_s, zp_r,
):
    place, across, sibling, after, before, at = partners()
    s_scale, s_bias, t_scale, t_bias = ss_ref[0], sb_ref[0], ts_ref[0], tb_ref[0]

    def remote(src, dst, ssem, rsem, dev):
        return pltpu.make_async_remote_copy(
            src_ref=src, dst_ref=dst, send_sem=ssem, recv_sem=rsem,
            device_id=dev, device_id_type=MESH,
        )

    loads = []
    for k, (r, m) in enumerate(CHUNKS):
        rows = pl.ds(r, m)
        loads.append([
            pltpu.make_async_copy(src.at[rows], dst.at[rows], in_sem.at[k, n])
            for n, (src, dst) in enumerate(
                ((ti_hbm, raw_ti), (si_hbm, raw_si), (tt_hbm, raw_tt), (st_hbm, raw_st))
            )
        ])
    for group in loads:
        for copy in group:
            copy.start()
    barrier = pltpu.get_barrier_semaphore()
    for dev in (across, sibling, before):
        pl.semaphore_signal(barrier, inc=1, device_id=dev, device_id_type=MESH)
    relays = place % HOP == 1

    @pl.when(place == 1 + HOP)
    def _():
        pl.semaphore_signal(barrier, inc=1, device_id=at(HOP, False), device_id_type=MESH)

    @pl.when(place == 1)
    def _():
        pl.semaphore_signal(barrier, inc=1, device_id=at(HOP - RUN, True), device_id_type=MESH)

    @pl.when(place == 0)
    def _():
        pl.semaphore_signal(barrier, inc=1, device_id=at(1, False), device_id_type=MESH)


    def unit(raw, rows, out, at, keep=None):
        wide = raw[rows].astype(jnp.float32)
        inverse = lax.rsqrt(jnp.sum(wide * wide, axis=-1, keepdims=True) + 1e-06)
        out[at] = (wide * inverse).astype(jnp.bfloat16)
        if keep is not None:
            keep[rows] = inverse

    def prev_at(k):
        r, m = CHUNKS[k]
        return pl.ds(OWN_TEXT + 2 * r, m), pl.ds(OWN_TEXT + 2 * r + m, m)

    y_cp, z_cp, d_cp, f_cp, far_cp = [], [], [], [], []
    for k, (r, m) in enumerate(CHUNKS):
        own = pl.ds(r, m)
        po, ps = prev_at(k)
        y_cp.append((
            remote(TI.at[own], TI.at[pl.ds(ROWS + r, m)], y_s.at[2 * k], y_r.at[2 * k], across),
            remote(SI.at[own], SI.at[pl.ds(ROWS + r, m)], y_s.at[2 * k + 1], y_r.at[2 * k + 1], across),
        ))
        z_cp.append((
            remote(TT.at[own], TT.at[po], z_s.at[2 * k], z_r.at[2 * k], after),
            remote(ST.at[own], ST.at[po], z_s.at[2 * k + 1], z_r.at[2 * k + 1], after),
        ))
        d_cp.append((
            remote(TT.at[own], TT.at[pl.ds(ROWS + r, m)], d_s.at[2 * k], d_r.at[2 * k], sibling),
            remote(ST.at[own], ST.at[pl.ds(ROWS + r, m)], d_s.at[2 * k + 1], d_r.at[2 * k + 1], sibling),
        ))
        f_cp.append((
            remote(TT.at[po], TT.at[ps], f_s.at[2 * k], f_r.at[2 * k], sibling),
            remote(ST.at[po], ST.at[ps], f_s.at[2 * k + 1], f_r.at[2 * k + 1], sibling),
        ))
        if k in FAR:
            down, over, home = at(-HOP, False), at(RUN - HOP, True), at(-1, False)
            stop = pl.ds(r - CHUNKS[FAR[0]][0], m)
            pairs = []
            for half, (text, stay) in enumerate(((TT, far_t), (ST, far_s))):
                n = 2 * (k - FAR[0]) + half
                pairs.append((
                    remote(text.at[own], stay.at[stop], q_s.at[n], q_r.at[n], down),
                    remote(stay.at[stop], stay.at[stop], q_s.at[n], q_r.at[n], over),
                    remote(stay.at[stop], text.at[po], q_s.at[n], z_r.at[2 * k + half], home),
                ))
            far_cp.extend(pairs)

    def pass_on(hop, first, last):
        @pl.when(place == 1 + HOP * (2 - hop))
        def _():
            for n in range(first, last):
                far_cp[n][0].wait_recv()
                far_cp[n][hop].start()

    def prepare_images(k):
        own = pl.ds(*CHUNKS[k])
        unit(raw_ti, own, TI, own)
        y_cp[k][0].start()
        unit(raw_si, own, SI, own, inv_i)
        y_cp[k][1].start()

    def prepare_text(k):
        own = pl.ds(*CHUNKS[k])
        unit(raw_tt, own, TT, own)
        unit(raw_st, own, ST, own, inv_t)

    for copy in loads[0]:
        copy.wait()
    own = pl.ds(*CHUNKS[0])
    unit(raw_ti, own, TI, own)
    unit(raw_tt, own, TT, own)
    pl.semaphore_wait(barrier, jnp.where(relays, 4, 3))
    y_cp[0][0].start()
    z_cp[0][0].start()
    unit(raw_si, own, SI, own, inv_i)
    unit(raw_st, own, ST, own, inv_t)
    y_cp[0][1].start()
    z_cp[0][1].start()
    d_cp[0][0].start()
    d_cp[0][1].start()
    for group in loads[1:]:
        for copy in group:
            copy.wait()
    for k in FAR:
        own = pl.ds(*CHUNKS[k])
        for half, norm in ((0, (raw_tt, own, TT, own)), (1, (raw_st, own, ST, own, inv_t))):
            unit(*norm)

            @pl.when(place == RUN - 1)
            def _():
                far_cp[2 * (k - FAR[0]) + half][0].start()
    for k in range(1, N_CH):
        if k not in FAR:
            prepare_text(k)
            for half in (0, 1):
                z_cp[k][half].start()
        for half in (0, 1):
            d_cp[k][half].start()

    @pl.when(place != RUN - 1)
    def _():
        for k in FAR:
            for half in (0, 1):
                z_cp[k][half].start()

    for k in range(1, N_CH):
        prepare_images(k)

    def teach(i, m, j, n):
        dot = lax.dot_general(TI[pl.ds(i, m)], TT[pl.ds(j, n)], NT, preferred_element_type=jnp.float32)
        TG[pl.ds(i, m), pl.ds(j, n)] = jax.nn.sigmoid(t_scale * dot + t_bias)

    def study(i, m, j, n):
        dot = lax.dot_general(SI[pl.ds(i, m)], ST[pl.ds(j, n)], NT, preferred_element_type=jnp.float32)
        at = (pl.ds(i, m), pl.ds(j, n))
        W[at] = (jax.nn.sigmoid(s_scale * dot + s_bias) - TG[at]).astype(jnp.bfloat16)

    teach(0, ROWS, 0, ROWS)
    study(0, ROWS, 0, ROWS)
    for k in range(N_CH):
        for copy in d_cp[k]:
            copy.wait_recv()
    teach(0, ROWS, ROWS, ROWS)
    study(0, ROWS, ROWS, ROWS)

    def arrive(k, half):
        z_cp[k][half].wait_recv()
        f_cp[k][half].start()

    def step(k):
        r, m = CHUNKS[k]
        j = OWN_TEXT + 2 * r
        for half, tile in ((0, teach), (1, study)):
            arrive(k, half)
            y_cp[k][half].wait_recv()
            if k == N_CH - 1 and half == 1:
                break
            tile(ROWS + r, m, 0, j)
            f_cp[k][half].wait_recv()
            tile(0, ROWS + r + m, j, 2 * m)
        for when, hop, first, last in RELAY:
            if when == k + 1:
                pass_on(hop, first, last)

    yp_cp = [
        remote(y_out.at[pl.ds(c * PULL, PULL)], y_in.at[pl.ds(c * PULL, PULL)], yp_s.at[c], yp_r.at[c], across)
        for c in range(N_PULL)
    ]
    zp_cp = [
        remote(z_out.at[pl.ds(r, m)], z_in.at[pl.ds(r, m)], zp_s.at[k], zp_r.at[k], before)
        for k, (r, m) in enumerate(CHUNKS)
    ]
    dp_cp = [
        remote(dp_out.at[pl.ds(r, m)], dp_in.at[pl.ds(r, m)], dp_s.at[k], dp_r.at[k], sibling)
        for k, (r, m) in enumerate(CHUNKS)
    ]
    dt_cp = remote(dt_out, dt_in, dt_s.at[0], dt_r.at[0], sibling)

    def image_pull(i, m):
        return jnp.dot(W[pl.ds(i, m), :], ST[...], preferred_element_type=jnp.float32)

    def text_pull(j, n):
        return lax.dot_general(W[:, pl.ds(j, n)], SI[...], TN, preferred_element_type=jnp.float32)

    def across_pull(c, n):
        y_out[pl.ds(c * PULL, n * PULL)] = image_pull(ROWS + c * PULL, n * PULL).astype(jnp.bfloat16)
        for i in range(c, c + n):
            yp_cp[i].start()

    def early_across(j):
        gi_ref[pl.ds(0, FIRST)] = jnp.dot(
            W[pl.ds(ROWS, FIRST), pl.ds(0, j)], ST[pl.ds(0, j)], preferred_element_type=jnp.float32
        )

    def late_across(j):
        rest = jnp.dot(
            W[pl.ds(ROWS, FIRST), pl.ds(j, 4 * ROWS - j)], ST[pl.ds(j, 4 * ROWS - j)],
            preferred_element_type=jnp.float32,
        )
        y_out[pl.ds(0, FIRST)] = (gi_ref[pl.ds(0, FIRST)] + rest).astype(jnp.bfloat16)
        for i in range(FIRST // PULL):
            yp_cp[i].start()

    def first_text(i, m):
        m0 = CHUNKS[0][1]
        return lax.dot_general(
            W[pl.ds(i, m), pl.ds(OWN_TEXT, 2 * m0)], SI[pl.ds(i, m)], TN, preferred_element_type=jnp.float32
        )

    def prev_leave(pull, first, last):
        r = CHUNKS[first][0]
        for k in range(first, last):
            at, m = CHUNKS[k]
            mine = 2 * (at - r)
            prev_own[pl.ds(at, m)] = pull[mine:mine + m]
            dp_out[pl.ds(at, m)] = pull[mine + m:mine + 2 * m].astype(jnp.bfloat16)
            dp_cp[k].start()

    def prev_pull(first, last):
        r, rows = CHUNKS[first][0], sum(m for _, m in CHUNKS[first:last])
        prev_leave(text_pull(OWN_TEXT + 2 * r, 2 * rows), first, last)

    def prev_send(k):
        r, m = CHUNKS[k]
        rows = pl.ds(r, m)
        dp_cp[k].wait_recv()
        z_out[rows] = (prev_own[rows] + dp_in[rows].astype(jnp.float32)).astype(jnp.bfloat16)
        zp_cp[k].start()

    @pl.when(place != 0)
    def _():
        pass_on(1, 0, 1)
        last = N_CH - 1
        for k in range(last):
            step(k)
        r, m = CHUNKS[last]
        j = OWN_TEXT + 2 * r
        early = pl.ds(0, 2 * CHUNKS[0][1])
        gt_ref[early] = first_text(0, ROWS + r)
        early_across(j)
        step(last)
        study(ROWS + r, m, OWN_TEXT, j - OWN_TEXT)
        prev_leave(gt_ref[early] + first_text(ROWS + r, m), 0, 1)
        study(ROWS + r, m, 0, OWN_TEXT)
        f_cp[last][1].wait_recv()
        study(0, 2 * ROWS, j, 2 * m)
        late_across(j)

    @pl.when(place == 0)
    def _():
        last = N_CH - 1
        r, m = CHUNKS[last]
        mid = CHUNKS[SPLIT][0]
        j = OWN_TEXT + 2 * mid
        for k in range(last):
            for half, tile in ((0, teach), (1, study)):
                y_cp[k][half].wait_recv()
                tile(ROWS + CHUNKS[k][0], CHUNKS[k][1], 0, OWN_TEXT)
            if k == 1:
                arrive(0, 0)
                arrive(0, 1)
        for k in (*range(1, SPLIT), *FAR[:-1]):
            arrive(k, 0)
            arrive(k, 1)
        for half, tile in ((0, teach), (1, study)):
            for k in range(SPLIT):
                f_cp[k][half].wait_recv()
            tile(0, ROWS + r, OWN_TEXT, j - OWN_TEXT)
        early_across(j)
        for half, tile in ((0, teach), (1, study)):
            for k in (*range(SPLIT, FAR[0]), last):
                arrive(k, half)
            y_cp[last][half].wait_recv()
            tile(ROWS + r, m, 0, j)
            if half == 1:
                prev_pull(0, 1)
            for k in range(SPLIT, N_CH):
                f_cp[k][half].wait_recv()
            tile(0, 2 * ROWS, j, 2 * (ROWS - mid))
        late_across(j)

    prev_send(0)
    prev_pull(1, 2)
    across_pull(2, 4)
    prev_send(1)
    prev_pull(2, N_CH)
    for k in range(2, N_CH):
        prev_send(k)
    dt_out[...] = text_pull(ROWS, ROWS).astype(jnp.bfloat16)
    dt_cp.start()
    img_own[...] = image_pull(0, ROWS)
    txt_own[...] = text_pull(0, ROWS)
    dt_cp.wait_recv()

    def project(pull, raw, inverse, scale):
        row = raw.astype(jnp.float32) * inverse
        grown = scale * pull
        return (grown - row * jnp.sum(row * grown, axis=-1, keepdims=True)) * inverse

    def finish_image(c):
        rows = pl.ds(c * PULL, PULL)
        yp_cp[c].wait_recv()
        pull = img_own[rows] + y_in[rows].astype(jnp.float32)
        gi_ref[rows] = project(pull, raw_si[rows], inv_i[rows], s_scale)

    def finish_text(k):
        r, m = CHUNKS[k]
        rows = pl.ds(r, m)
        zp_cp[k].wait_recv()
        pull = txt_own[rows] + dt_in[rows].astype(jnp.float32) + z_in[rows].astype(jnp.float32)
        gt_ref[rows] = project(pull, raw_st[rows], inv_t[rows], s_scale)

    for image, text in ((0, 0), (1, None), (2, 1), (3, 2), (4, 3), (5, 4)):
        finish_image(image)
        if text is not None:
            finish_text(text)

    for n, copies in enumerate(far_cp):
        @pl.when(relays)
        def _():
            copies[0].wait_send()

        @pl.when(place != RUN - 1)
        def _():
            z_cp[FAR[n // 2]][n % 2].wait_send()

    near = [z_cp[k] for k in range(N_CH) if k not in FAR]
    for group in (*y_cp, *near, *d_cp, *f_cp, yp_cp, zp_cp, dp_cp, (dt_cp,)):
        for copy in group:
            copy.wait_send()


def write_kernel(gi_ref, gt_ref, gi_hbm, gt_hbm, sem):
    copies = []
    for k in range(N_WRITE):
        rows = pl.ds(k * (ROWS // N_WRITE), ROWS // N_WRITE)
        for n, (src, dst) in enumerate(((gi_ref, gi_hbm), (gt_ref, gt_hbm))):
            copies.append(pltpu.make_async_copy(src.at[rows], dst.at[rows], sem.at[k, n]))
    for copy in copies:
        copy.start()
    for copy in copies:
        copy.wait()


def per_device(si, st, ti, tt, ss, sb, ts, tb):
    half, full = jnp.bfloat16, jnp.float32
    dma = pltpu.SemaphoreType.DMA
    smem = pl.BlockSpec(memory_space=pltpu.SMEM)
    hbm = pl.BlockSpec(memory_space=pltpu.HBM)
    free = pl.BlockSpec(memory_space=pl.ANY)
    part = lambda dtype: pltpu.VMEM((ROWS, D_S), dtype)
    grads = pl.pallas_call(
        kernel,
        out_shape=(jax.ShapeDtypeStruct((ROWS, D_S), full),) * 2,
        in_specs=[smem] * 4 + [hbm] * 4,
        out_specs=(pl.BlockSpec(memory_space=pltpu.VMEM),) * 2,
        scratch_shapes=[
            part(half), part(half), pltpu.VMEM((ROWS, D_T), half), pltpu.VMEM((ROWS, D_T), half),
            pltpu.VMEM((ROWS, 1), full), pltpu.VMEM((ROWS, 1), full),
            pltpu.VMEM((2 * ROWS, D_S), half), pltpu.VMEM((2 * ROWS, D_T), half),
            pltpu.VMEM((4 * ROWS, D_S), half), pltpu.VMEM((4 * ROWS, D_T), half),
            pltpu.VMEM((2 * ROWS, 4 * ROWS), full), pltpu.VMEM((2 * ROWS, 4 * ROWS), half),
            part(full), part(full), part(full),
            *[part(half)] * 8,
            pltpu.VMEM((FAR_ROWS, D_T), half), pltpu.VMEM((FAR_ROWS, D_S), half),
            dma((N_CH, 4)),
            dma((2 * len(FAR),)), dma((2 * len(FAR),)),
            *[dma((2 * N_CH,))] * 8,
            dma((N_PULL,)), dma((N_PULL,)), dma((1,)), dma((1,)),
            *[dma((N_CH,))] * 4,
        ],
        compiler_params=pltpu.CompilerParams(
            collective_id=0, has_side_effects=True, vmem_limit_bytes=44 * 2**20,
        ),
    )(ss, sb, ts, tb, *[pltpu.with_memory_space_constraint(x, pltpu.HBM) for x in (si, st, ti, tt)])
    return pl.pallas_call(
        write_kernel,
        out_shape=(jax.ShapeDtypeStruct((ROWS, D_S), full),) * 2,
        in_specs=[free, free],
        out_specs=(hbm, hbm),
        scratch_shapes=[dma((N_WRITE, 2))],
        compiler_params=pltpu.CompilerParams(vmem_limit_bytes=2**20),
    )(*grads)


def solution(mesh):
    row = P(("loop", "grp"), None)
    return jax.shard_map(
        per_device,
        mesh=mesh,
        in_specs=(row, row, row, row, P(), P(), P(), P()),
        out_specs=(row, row),
        check_vma=False,
    )
```

```python
import functools

import jax
import jax.numpy as jnp
from jax import lax
from jax.experimental import pallas as pl
from jax.experimental.pallas import tpu as pltpu
from jax.sharding import PartitionSpec as P

MESH = pl.DeviceIdType.MESH
N_LOOP = 64
HOP = 3
RUN = 2 * HOP + 2
ROWS = 384
D_S = 768
D_T = 1152
CHUNKS = ((0, 64), (64, 128), (192, 64), (256, 64), (320, 64))
N_CH = len(CHUNKS)
FAR = (3, 4)
FAR_ROWS = 128
SPLIT = 2
RELAY = ((1, 1, 1, 4), (1, 2, 0, 1), (2, 2, 1, 2), (3, 2, 2, 4))
N_WRITE = 2
PULL = 64
FIRST = 2 * PULL
N_PULL = ROWS // PULL
OWN_TEXT = 2 * ROWS

NT = (((1,), (1,)), ((), ()))
TN = (((0,), (0,)), ((), ()))


def partners():
    loop = lax.axis_index("loop")
    grp = lax.axis_index("grp")
    chip = grp // 2
    core = grp % 2
    place = loop % RUN
    swapped = (1 - chip) * 2 + core

    def at(step, swap):
        side = jnp.where(swap, swapped, grp)
        return ((loop + step + N_LOOP) % N_LOOP, side)

    across = (loop, swapped)
    sibling = (loop, chip * 2 + 1 - core)
    after = at(1, place == RUN - 1)
    before = at(-1, place == 0)
    return core, place, across, sibling, after, before, at


def kernel(
    ss_ref, sb_ref, ts_ref, tb_ref, si_hbm, st_hbm, ti_hbm, tt_hbm, gi_ref, gt_ref,
    raw_si, raw_st, raw_ti, raw_tt, inv_i, inv_t,
    SI, TI, ST, TT, TG, W,
    img_own, txt_own, prev_own,
    y_out, y_in, dt_out, dt_in, dp_out, dp_in, z_out, z_in,
    far_t, far_s,
    gate, in_sem,
    q_s, q_r,
    y_s, y_r, z_s, z_r, d_s, d_r, f_s, f_r,
    yp_s, yp_r, dt_s, dt_r, dp_s, dp_r, zp_s, zp_r,
):
    core, place, across, sibling, after, before, at = partners()
    s_scale, s_bias, t_scale, t_bias = ss_ref[0], sb_ref[0], ts_ref[0], tb_ref[0]

    def remote(src, dst, ssem, rsem, dev):
        return pltpu.make_async_remote_copy(
            src_ref=src, dst_ref=dst, send_sem=ssem, recv_sem=rsem,
            device_id=dev, device_id_type=MESH,
        )

    loads = [
        [
            pltpu.make_async_copy(src.at[pl.ds(r, m)], dst.at[pl.ds(r, m)], in_sem.at[k, n])
            for n, (src, dst) in enumerate(
                ((ti_hbm, raw_ti), (tt_hbm, raw_tt), (si_hbm, raw_si), (st_hbm, raw_st))
            )
        ]
        for k, (r, m) in enumerate((CHUNKS[0], (CHUNKS[1][0], ROWS - CHUNKS[1][0])))
    ]
    for group in loads:
        for copy in group:
            copy.start()
    barrier = pltpu.get_barrier_semaphore()
    relays = place % HOP == 1

    def report(dev, to):
        pl.semaphore_signal(barrier, inc=1, device_id=(dev[0], dev[1] // 2 * 2 + to), device_id_type=MESH)

    report(across, 0)
    report(before, 1)

    @pl.when(core == 1)
    def _():
        report(sibling, 0)

    @pl.when(place == 1 + HOP)
    def _():
        report(at(HOP, False), 1)

    @pl.when(place == 1)
    def _():
        report(at(HOP - RUN, True), 1)

    @pl.when(place == 0)
    def _():
        report(at(1, False), 1)

    def wait_gate(counter, amount):
        @pl.when(core == counter)
        def _():
            pl.semaphore_wait(barrier, amount)
            pl.semaphore_signal(gate, inc=1, device_id=sibling, device_id_type=MESH)

        @pl.when(core != counter)
        def _():
            pl.semaphore_wait(gate, 1)

    def unit(raw, rows, out, at, keep=None):
        wide = raw[rows].astype(jnp.float32)
        inverse = lax.rsqrt(jnp.sum(wide * wide, axis=-1, keepdims=True) + 1e-06)
        out[at] = (wide * inverse).astype(jnp.bfloat16)
        if keep is not None:
            keep[rows] = inverse

    def prev_at(k):
        r, m = CHUNKS[k]
        return pl.ds(OWN_TEXT + 2 * r, m), pl.ds(OWN_TEXT + 2 * r + m, m)

    y_cp, z_cp, d_cp, f_cp, far_cp = [], [], [], [], []
    for k, (r, m) in enumerate(CHUNKS):
        own = pl.ds(r, m)
        po, ps = prev_at(k)
        y_cp.append((
            remote(TI.at[own], TI.at[pl.ds(ROWS + r, m)], y_s.at[0], y_r.at[2 * k], across),
            remote(SI.at[own], SI.at[pl.ds(ROWS + r, m)], y_s.at[1], y_r.at[2 * k + 1], across),
        ))
        z_cp.append((
            remote(TT.at[own], TT.at[po], z_s.at[2 * (k in FAR)], z_r.at[2 * k], after),
            remote(ST.at[own], ST.at[po], z_s.at[2 * (k in FAR) + 1], z_r.at[2 * k + 1], after),
        ))
        d_cp.append((
            remote(TT.at[own], TT.at[pl.ds(ROWS + r, m)], d_s.at[0], d_r.at[0], sibling),
            remote(ST.at[own], ST.at[pl.ds(ROWS + r, m)], d_s.at[1], d_r.at[1], sibling),
        ))
        f_cp.append((
            remote(TT.at[po], TT.at[ps], f_s.at[0], f_r.at[2 * k], sibling),
            remote(ST.at[po], ST.at[ps], f_s.at[1], f_r.at[2 * k + 1], sibling),
        ))
        if k in FAR:
            down, over, home = at(-HOP, False), at(RUN - HOP, True), at(-1, False)
            stop = pl.ds(r - CHUNKS[FAR[0]][0], m)
            pairs = []
            for half, (text, stay) in enumerate(((TT, far_t), (ST, far_s))):
                n = 2 * (k - FAR[0]) + half
                pairs.append((
                    remote(text.at[own], stay.at[stop], q_s.at[half], q_r.at[n], down),
                    remote(stay.at[stop], stay.at[stop], q_s.at[half], q_r.at[n], over),
                    remote(stay.at[stop], text.at[po], q_s.at[half], z_r.at[2 * k + half], home),
                ))
            far_cp.extend(pairs)

    def pass_on(hop, first, last):
        @pl.when(place == 1 + HOP * (2 - hop))
        def _():
            for n in range(first, last):
                far_cp[n][0].wait_recv()
                far_cp[n][hop].start()

    def prepare_images(k):
        own = pl.ds(*CHUNKS[k])
        unit(raw_ti, own, TI, own)
        y_cp[k][0].start()
        unit(raw_si, own, SI, own, inv_i)
        y_cp[k][1].start()

    def prepare_text(k):
        own = pl.ds(*CHUNKS[k])
        unit(raw_tt, own, TT, own)
        unit(raw_st, own, ST, own, inv_t)

    for copy in loads[0]:
        copy.wait()
    own = pl.ds(*CHUNKS[0])
    unit(raw_ti, own, TI, own)
    unit(raw_si, own, SI, own, inv_i)
    wait_gate(0, 3)
    for half in (0, 1):
        y_cp[0][half].start()
    unit(raw_tt, own, TT, own)
    unit(raw_st, own, ST, own, inv_t)
    for half in (0, 1):
        d_cp[0][half].start()
    for copy in loads[1]:
        copy.wait()
    wait_gate(1, jnp.where(relays, 4, 2))
    for half in (0, 1):
        z_cp[0][half].start()
    for k in FAR:
        own = pl.ds(*CHUNKS[k])
        for half, norm in ((0, (raw_tt, own, TT, own)), (1, (raw_st, own, ST, own, inv_t))):
            unit(*norm)

            @pl.when(place == RUN - 1)
            def _():
                far_cp[2 * (k - FAR[0]) + half][0].start()
    for k in range(1, N_CH):
        if k not in FAR:
            prepare_text(k)
            for half in (0, 1):
                z_cp[k][half].start()
        for half in (0, 1):
            d_cp[k][half].start()

    @pl.when(place != RUN - 1)
    def _():
        for k in FAR:
            for half in (0, 1):
                z_cp[k][half].start()

    for k in range(1, N_CH):
        prepare_images(k)

    def teach(i, m, j, n):
        dot = lax.dot_general(TI[pl.ds(i, m)], TT[pl.ds(j, n)], NT, preferred_element_type=jnp.float32)
        TG[pl.ds(i, m), pl.ds(j, n)] = jax.nn.sigmoid(t_scale * dot + t_bias)

    def study(i, m, j, n):
        dot = lax.dot_general(SI[pl.ds(i, m)], ST[pl.ds(j, n)], NT, preferred_element_type=jnp.float32)
        at = (pl.ds(i, m), pl.ds(j, n))
        W[at] = (jax.nn.sigmoid(s_scale * dot + s_bias) - TG[at]).astype(jnp.bfloat16)

    teach(0, ROWS, 0, ROWS)
    study(0, ROWS, 0, ROWS)
    for half, text in enumerate((TT, ST)):
        theirs = text.at[pl.ds(ROWS, ROWS)]
        remote(theirs, theirs, d_s.at[half], d_r.at[half], sibling).wait_recv()
    teach(0, ROWS, ROWS, ROWS)
    study(0, ROWS, ROWS, ROWS)

    def arrive(k, half):
        z_cp[k][half].wait_recv()
        f_cp[k][half].start()

    def step(k):
        r, m = CHUNKS[k]
        j = OWN_TEXT + 2 * r
        for half, tile in ((0, teach), (1, study)):
            arrive(k, half)
            y_cp[k][half].wait_recv()
            if k == N_CH - 1 and half == 1:
                break
            tile(ROWS + r, m, 0, j)
            f_cp[k][half].wait_recv()
            tile(0, ROWS + r + m, j, 2 * m)
        for when, hop, first, last in RELAY:
            if when == k + 1:
                pass_on(hop, first, last)

    yp_cp = [
        remote(y_out.at[pl.ds(c * PULL, PULL)], y_in.at[pl.ds(c * PULL, PULL)], yp_s.at[0], yp_r.at[c], across)
        for c in range(N_PULL)
    ]
    zp_cp = [
        remote(z_out.at[pl.ds(r, m)], z_in.at[pl.ds(r, m)], zp_s.at[0], zp_r.at[k], before)
        for k, (r, m) in enumerate(CHUNKS)
    ]
    dp_cp = [
        remote(dp_out.at[pl.ds(r, m)], dp_in.at[pl.ds(r, m)], dp_s.at[0], dp_r.at[k], sibling)
        for k, (r, m) in enumerate(CHUNKS)
    ]
    dt_cp = remote(dt_out, dt_in, dt_s.at[0], dt_r.at[0], sibling)

    def image_pull(i, m):
        return jnp.dot(W[pl.ds(i, m), :], ST[...], preferred_element_type=jnp.float32)

    def text_pull(j, n):
        return lax.dot_general(W[:, pl.ds(j, n)], SI[...], TN, preferred_element_type=jnp.float32)

    def across_pull(c, n):
        y_out[pl.ds(c * PULL, n * PULL)] = image_pull(ROWS + c * PULL, n * PULL).astype(jnp.bfloat16)
        for i in range(c, c + n):
            yp_cp[i].start()

    def early_across(j):
        gi_ref[pl.ds(0, FIRST)] = jnp.dot(
            W[pl.ds(ROWS, FIRST), pl.ds(0, j)], ST[pl.ds(0, j)], preferred_element_type=jnp.float32
        )

    def late_across(j):
        rest = jnp.dot(
            W[pl.ds(ROWS, FIRST), pl.ds(j, 4 * ROWS - j)], ST[pl.ds(j, 4 * ROWS - j)],
            preferred_element_type=jnp.float32,
        )
        y_out[pl.ds(0, FIRST)] = (gi_ref[pl.ds(0, FIRST)] + rest).astype(jnp.bfloat16)
        for i in range(FIRST // PULL):
            yp_cp[i].start()

    def first_text(i, m):
        m0 = CHUNKS[0][1]
        return lax.dot_general(
            W[pl.ds(i, m), pl.ds(OWN_TEXT, 2 * m0)], SI[pl.ds(i, m)], TN, preferred_element_type=jnp.float32
        )

    def prev_leave(pull, first, last):
        r = CHUNKS[first][0]
        for k in range(first, last):
            at, m = CHUNKS[k]
            mine = 2 * (at - r)
            prev_own[pl.ds(at, m)] = pull[mine:mine + m]
            dp_out[pl.ds(at, m)] = pull[mine + m:mine + 2 * m].astype(jnp.bfloat16)
            dp_cp[k].start()

    def prev_pull(first, last):
        r, rows = CHUNKS[first][0], sum(m for _, m in CHUNKS[first:last])
        prev_leave(text_pull(OWN_TEXT + 2 * r, 2 * rows), first, last)

    def prev_send(k):
        r, m = CHUNKS[k]
        rows = pl.ds(r, m)
        dp_cp[k].wait_recv()
        z_out[rows] = (prev_own[rows] + dp_in[rows].astype(jnp.float32)).astype(jnp.bfloat16)
        zp_cp[k].start()

    @pl.when(place != 0)
    def _():
        pass_on(1, 0, 1)
        last = N_CH - 1
        for k in range(last):
            step(k)
        r, m = CHUNKS[last]
        j = OWN_TEXT + 2 * r
        early = pl.ds(0, 2 * CHUNKS[0][1])
        gt_ref[early] = first_text(0, ROWS + r)
        early_across(j)
        step(last)
        study(ROWS + r, m, OWN_TEXT, j - OWN_TEXT)
        prev_leave(gt_ref[early] + first_text(ROWS + r, m), 0, 1)
        study(ROWS + r, m, 0, OWN_TEXT)
        f_cp[last][1].wait_recv()
        study(0, 2 * ROWS, j, 2 * m)
        late_across(j)

    @pl.when(place == 0)
    def _():
        last = N_CH - 1
        r, m = CHUNKS[last]
        mid = CHUNKS[SPLIT][0]
        j = OWN_TEXT + 2 * mid
        for k in range(last):
            for half, tile in ((0, teach), (1, study)):
                y_cp[k][half].wait_recv()
                tile(ROWS + CHUNKS[k][0], CHUNKS[k][1], 0, OWN_TEXT)
            if k == 1:
                arrive(0, 0)
                arrive(0, 1)
        for k in (*range(1, SPLIT), *FAR[:-1]):
            arrive(k, 0)
            arrive(k, 1)
        for half, tile in ((0, teach), (1, study)):
            for k in range(SPLIT):
                f_cp[k][half].wait_recv()
            tile(0, ROWS + r, OWN_TEXT, j - OWN_TEXT)
        early_across(j)
        for half, tile in ((0, teach), (1, study)):
            for k in (*range(SPLIT, FAR[0]), last):
                arrive(k, half)
            y_cp[last][half].wait_recv()
            tile(ROWS + r, m, 0, j)
            if half == 1:
                prev_pull(0, 1)
            for k in range(SPLIT, N_CH):
                f_cp[k][half].wait_recv()
            tile(0, 2 * ROWS, j, 2 * (ROWS - mid))
        late_across(j)

    prev_send(0)
    prev_pull(1, 2)
    across_pull(2, 4)
    prev_send(1)
    prev_pull(2, N_CH)
    for k in range(2, N_CH):
        prev_send(k)
    dt_out[...] = text_pull(ROWS, ROWS).astype(jnp.bfloat16)
    dt_cp.start()
    img_own[...] = image_pull(0, ROWS)
    txt_own[...] = text_pull(0, ROWS)
    dt_cp.wait_recv()

    def project(pull, raw, inverse, scale):
        row = raw.astype(jnp.float32) * inverse
        grown = scale * pull
        return (grown - row * jnp.sum(row * grown, axis=-1, keepdims=True)) * inverse

    def finish_image(c):
        rows = pl.ds(c * PULL, PULL)
        yp_cp[c].wait_recv()
        pull = img_own[rows] + y_in[rows].astype(jnp.float32)
        gi_ref[rows] = project(pull, raw_si[rows], inv_i[rows], s_scale)

    def finish_text(k):
        r, m = CHUNKS[k]
        rows = pl.ds(r, m)
        zp_cp[k].wait_recv()
        pull = txt_own[rows] + dt_in[rows].astype(jnp.float32) + z_in[rows].astype(jnp.float32)
        gt_ref[rows] = project(pull, raw_st[rows], inv_t[rows], s_scale)

    for image, text in ((0, 0), (1, None), (2, 1), (3, 2), (4, 3), (5, 4)):
        finish_image(image)
        if text is not None:
            finish_text(text)

    near = CHUNKS[FAR[0]][0]
    sent = [
        (y_out, yp_s.at[0]), (z_out, zp_s.at[0]), (dp_out, dp_s.at[0]), (dt_out, dt_s.at[0]),
    ]
    for half, (image, text) in enumerate(((TI, TT), (SI, ST))):
        whole = pl.ds(0, ROWS)
        sent += [(image.at[whole], y_s.at[half]), (text.at[whole], d_s.at[half]), (text.at[whole], f_s.at[half])]
        sent += [(text.at[pl.ds(0, near)], z_s.at[half])]
    for src, sem in sent:
        remote(src, src, sem, sem, sibling).wait_send()

    @pl.when(relays)
    def _():
        for half, stay in enumerate((far_t, far_s)):
            remote(stay, stay, q_s.at[half], q_s.at[half], sibling).wait_send()

    @pl.when(place != RUN - 1)
    def _():
        for half, text in enumerate((TT, ST)):
            rows = text.at[pl.ds(near, ROWS - near)]
            remote(rows, rows, z_s.at[2 + half], z_s.at[2 + half], sibling).wait_send()


def write_kernel(gi_ref, gt_ref, gi_hbm, gt_hbm, sem):
    copies = []
    for k in range(N_WRITE):
        rows = pl.ds(k * (ROWS // N_WRITE), ROWS // N_WRITE)
        for n, (src, dst) in enumerate(((gi_ref, gi_hbm), (gt_ref, gt_hbm))):
            copies.append(pltpu.make_async_copy(src.at[rows], dst.at[rows], sem.at[k, n]))
    for copy in copies:
        copy.start()
    for copy in copies:
        copy.wait()


def per_device(si, st, ti, tt, ss, sb, ts, tb):
    half, full = jnp.bfloat16, jnp.float32
    dma = pltpu.SemaphoreType.DMA
    smem = pl.BlockSpec(memory_space=pltpu.SMEM)
    hbm = pl.BlockSpec(memory_space=pltpu.HBM)
    free = pl.BlockSpec(memory_space=pl.ANY)
    part = lambda dtype: pltpu.VMEM((ROWS, D_S), dtype)
    grads = pl.pallas_call(
        kernel,
        out_shape=(jax.ShapeDtypeStruct((ROWS, D_S), full),) * 2,
        in_specs=[smem] * 4 + [hbm] * 4,
        out_specs=(pl.BlockSpec(memory_space=pltpu.VMEM),) * 2,
        scratch_shapes=[
            part(half), part(half), pltpu.VMEM((ROWS, D_T), half), pltpu.VMEM((ROWS, D_T), half),
            pltpu.VMEM((ROWS, 1), full), pltpu.VMEM((ROWS, 1), full),
            pltpu.VMEM((2 * ROWS, D_S), half), pltpu.VMEM((2 * ROWS, D_T), half),
            pltpu.VMEM((4 * ROWS, D_S), half), pltpu.VMEM((4 * ROWS, D_T), half),
            pltpu.VMEM((2 * ROWS, 4 * ROWS), full), pltpu.VMEM((2 * ROWS, 4 * ROWS), half),
            part(full), part(full), part(full),
            *[part(half)] * 8,
            pltpu.VMEM((FAR_ROWS, D_T), half), pltpu.VMEM((FAR_ROWS, D_S), half),
            pltpu.SemaphoreType.REGULAR, dma((2, 4)),
            dma((2,)), dma((2 * len(FAR),)),
            dma((2,)), dma((2 * N_CH,)), dma((4,)), dma((2 * N_CH,)), dma((2,)), dma((2,)), dma((2,)), dma((2 * N_CH,)),
            dma((1,)), dma((N_PULL,)), dma((1,)), dma((1,)), dma((1,)), dma((N_CH,)), dma((1,)), dma((N_CH,)),
        ],
        compiler_params=pltpu.CompilerParams(
            collective_id=0, has_side_effects=True, vmem_limit_bytes=44 * 2**20,
        ),
    )(ss, sb, ts, tb, *[pltpu.with_memory_space_constraint(x, pltpu.HBM) for x in (si, st, ti, tt)])
    return pl.pallas_call(
        write_kernel,
        out_shape=(jax.ShapeDtypeStruct((ROWS, D_S), full),) * 2,
        in_specs=[free, free],
        out_specs=(hbm, hbm),
        scratch_shapes=[dma((N_WRITE, 2))],
        compiler_params=pltpu.CompilerParams(vmem_limit_bytes=2**20),
    )(*grads)


def solution(mesh):
    row = P(("loop", "grp"), None)
    return jax.shard_map(
        per_device,
        mesh=mesh,
        in_specs=(row, row, row, row, P(), P(), P(), P()),
        out_specs=(row, row),
        check_vma=False,
    )
```

```python
import functools

import jax
import jax.numpy as jnp
from jax import lax
from jax.experimental import pallas as pl
from jax.experimental.pallas import tpu as pltpu
from jax.sharding import PartitionSpec as P

MESH = pl.DeviceIdType.MESH
N_LOOP = 64
HOP = 3
RUN = 2 * HOP + 2
ROWS = 384
D_S = 768
D_T = 1152
CHUNKS = ((0, 64), (64, 128), (192, 64), (256, 64), (320, 64))
N_CH = len(CHUNKS)
FAR = (3, 4)
FAR_ROWS = 128
SPLIT = 2
RELAY = ((1, 1, 1, 4), (1, 2, 0, 1), (2, 2, 1, 2), (3, 2, 2, 4))
N_WRITE = 2
PULL = 64
FIRST = 2 * PULL
N_PULL = ROWS // PULL
OWN_TEXT = 2 * ROWS

NT = (((1,), (1,)), ((), ()))
TN = (((0,), (0,)), ((), ()))


def partners():
    loop = lax.axis_index("loop")
    grp = lax.axis_index("grp")
    chip = grp // 2
    core = grp % 2
    place = loop % RUN
    swapped = (1 - chip) * 2 + core

    def at(step, swap):
        side = jnp.where(swap, swapped, grp)
        return ((loop + step + N_LOOP) % N_LOOP, side)

    across = (loop, swapped)
    sibling = (loop, chip * 2 + 1 - core)
    after = at(1, place == RUN - 1)
    before = at(-1, place == 0)
    return core, place, across, sibling, after, before, at


def kernel(
    ss_ref, sb_ref, ts_ref, tb_ref, si_hbm, st_hbm, ti_hbm, tt_hbm, gi_ref, gt_ref,
    raw_si, raw_st, raw_ti, raw_tt, inv_i, inv_t,
    SI, TI, ST, TT, TG, W,
    img_own, txt_own, prev_own,
    y_out, y_in, dt_out, dt_in, dp_out, dp_in, z_out, z_in,
    far_t, far_s,
    gate, in_sem,
    q_s, q_r,
    y_s, y_r, z_s, z_r, d_s, d_r, f_s, f_r,
    yp_s, yp_r, dt_s, dt_r, dp_s, dp_r, zp_s, zp_r,
):
    core, place, across, sibling, after, before, at = partners()
    s_scale, s_bias, t_scale, t_bias = ss_ref[0], sb_ref[0], ts_ref[0], tb_ref[0]

    def remote(src, dst, ssem, rsem, dev):
        return pltpu.make_async_remote_copy(
            src_ref=src, dst_ref=dst, send_sem=ssem, recv_sem=rsem,
            device_id=dev, device_id_type=MESH,
        )

    loads = [
        [
            pltpu.make_async_copy(src.at[pl.ds(r, m)], dst.at[pl.ds(r, m)], in_sem.at[k, n])
            for n, (src, dst) in enumerate(
                ((ti_hbm, raw_ti), (tt_hbm, raw_tt), (si_hbm, raw_si), (st_hbm, raw_st))
            )
        ]
        for k, (r, m) in enumerate((CHUNKS[0], (CHUNKS[1][0], ROWS - CHUNKS[1][0])))
    ]
    for group in loads:
        for copy in group:
            copy.start()
    barrier = pltpu.get_barrier_semaphore()
    relays = place % HOP == 1

    def report(dev, to):
        pl.semaphore_signal(barrier, inc=1, device_id=(dev[0], dev[1] // 2 * 2 + to), device_id_type=MESH)

    report(across, 0)
    report(before, 1)

    @pl.when(core == 1)
    def _():
        report(sibling, 0)

    @pl.when(place == 1 + HOP)
    def _():
        report(at(HOP, False), 1)

    @pl.when(place == 1)
    def _():
        report(at(HOP - RUN, True), 1)

    @pl.when(place == 0)
    def _():
        report(at(1, False), 1)

    def wait_gate(counter, amount):
        @pl.when(core == counter)
        def _():
            pl.semaphore_wait(barrier, amount)
            pl.semaphore_signal(gate, inc=1, device_id=sibling, device_id_type=MESH)

        @pl.when(core != counter)
        def _():
            pl.semaphore_wait(gate, 1)

    def unit(raw, rows, out, at, keep=None):
        wide = raw[rows].astype(jnp.float32)
        inverse = lax.rsqrt(jnp.sum(wide * wide, axis=-1, keepdims=True) + 1e-06)
        out[at] = (wide * inverse).astype(jnp.bfloat16)
        if keep is not None:
            keep[rows] = inverse

    def prev_at(k):
        r, m = CHUNKS[k]
        return pl.ds(OWN_TEXT + 2 * r, m), pl.ds(OWN_TEXT + 2 * r + m, m)

    y_cp, z_cp, d_cp, f_cp, far_cp = [], [], [], [], []
    for k, (r, m) in enumerate(CHUNKS):
        own = pl.ds(r, m)
        po, ps = prev_at(k)
        y_cp.append((
            remote(TI.at[own], TI.at[pl.ds(ROWS + r, m)], y_s.at[0], y_r.at[2 * k], across),
            remote(SI.at[own], SI.at[pl.ds(ROWS + r, m)], y_s.at[1], y_r.at[2 * k + 1], across),
        ))
        z_cp.append((
            remote(TT.at[own], TT.at[po], z_s.at[2 * (k in FAR)], z_r.at[2 * k], after),
            remote(ST.at[own], ST.at[po], z_s.at[2 * (k in FAR) + 1], z_r.at[2 * k + 1], after),
        ))
        d_cp.append((
            remote(TT.at[own], TT.at[pl.ds(ROWS + r, m)], d_s.at[0], d_r.at[0], sibling),
            remote(ST.at[own], ST.at[pl.ds(ROWS + r, m)], d_s.at[1], d_r.at[1], sibling),
        ))
        f_cp.append((
            remote(TT.at[po], TT.at[ps], f_s.at[0], f_r.at[2 * k], sibling),
            remote(ST.at[po], ST.at[ps], f_s.at[1], f_r.at[2 * k + 1], sibling),
        ))
        if k in FAR:
            down, over, home = at(-HOP, False), at(RUN - HOP, True), at(-1, False)
            stop = pl.ds(r - CHUNKS[FAR[0]][0], m)
            pairs = []
            for half, (text, stay) in enumerate(((TT, far_t), (ST, far_s))):
                n = 2 * (k - FAR[0]) + half
                pairs.append((
                    remote(text.at[own], stay.at[stop], q_s.at[half], q_r.at[n], down),
                    remote(stay.at[stop], stay.at[stop], q_s.at[half], q_r.at[n], over),
                    remote(stay.at[stop], text.at[po], q_s.at[half], z_r.at[2 * k + half], home),
                ))
            far_cp.extend(pairs)

    def pass_on(hop, first, last):
        @pl.when(place == 1 + HOP * (2 - hop))
        def _():
            for n in range(first, last):
                far_cp[n][0].wait_recv()
                far_cp[n][hop].start()

    def prepare_images(k):
        own = pl.ds(*CHUNKS[k])
        unit(raw_ti, own, TI, own)
        y_cp[k][0].start()
        unit(raw_si, own, SI, own, inv_i)
        y_cp[k][1].start()

    def prepare_text(k):
        own = pl.ds(*CHUNKS[k])
        unit(raw_tt, own, TT, own)
        unit(raw_st, own, ST, own, inv_t)

    for copy in loads[0]:
        copy.wait()
    own = pl.ds(*CHUNKS[0])
    unit(raw_ti, own, TI, own)
    unit(raw_si, own, SI, own, inv_i)
    wait_gate(0, 3)
    for half in (0, 1):
        y_cp[0][half].start()
    unit(raw_tt, own, TT, own)
    unit(raw_st, own, ST, own, inv_t)
    for half in (0, 1):
        d_cp[0][half].start()
    for copy in loads[1]:
        copy.wait()
    wait_gate(1, jnp.where(relays, 4, 2))
    for half in (0, 1):
        z_cp[0][half].start()
    for k in FAR:
        own = pl.ds(*CHUNKS[k])
        for half, norm in ((0, (raw_tt, own, TT, own)), (1, (raw_st, own, ST, own, inv_t))):
            unit(*norm)

            @pl.when(place == RUN - 1)
            def _():
                far_cp[2 * (k - FAR[0]) + half][0].start()
    for k in range(1, N_CH):
        if k not in FAR:
            prepare_text(k)
            for half in (0, 1):
                z_cp[k][half].start()
        for half in (0, 1):
            d_cp[k][half].start()

    @pl.when(place != RUN - 1)
    def _():
        for k in FAR:
            for half in (0, 1):
                z_cp[k][half].start()

    for k in range(1, N_CH):
        prepare_images(k)

    def teach(i, m, j, n):
        dot = lax.dot_general(TI[pl.ds(i, m)], TT[pl.ds(j, n)], NT, preferred_element_type=jnp.float32)
        TG[pl.ds(i, m), pl.ds(j, n)] = jax.nn.sigmoid(t_scale * dot + t_bias)

    def study(i, m, j, n):
        dot = lax.dot_general(SI[pl.ds(i, m)], ST[pl.ds(j, n)], NT, preferred_element_type=jnp.float32)
        at = (pl.ds(i, m), pl.ds(j, n))
        W[at] = (jax.nn.sigmoid(s_scale * dot + s_bias) - TG[at]).astype(jnp.bfloat16)

    teach(0, ROWS, 0, ROWS)
    study(0, ROWS, 0, ROWS)
    for half, text in enumerate((TT, ST)):
        theirs = text.at[pl.ds(ROWS, ROWS)]
        remote(theirs, theirs, d_s.at[half], d_r.at[half], sibling).wait_recv()
    teach(0, ROWS, ROWS, ROWS)
    study(0, ROWS, ROWS, ROWS)

    def arrive(k, half):
        z_cp[k][half].wait_recv()
        f_cp[k][half].start()

    def step(k):
        r, m = CHUNKS[k]
        j = OWN_TEXT + 2 * r
        for half, tile in ((0, teach), (1, study)):
            arrive(k, half)
            y_cp[k][half].wait_recv()
            if k == N_CH - 1 and half == 1:
                break
            tile(ROWS + r, m, 0, j)
            f_cp[k][half].wait_recv()
            tile(0, ROWS + r + m, j, 2 * m)
        for when, hop, first, last in RELAY:
            if when == k + 1:
                pass_on(hop, first, last)

    yp_cp = [
        remote(y_out.at[pl.ds(c * PULL, PULL)], y_in.at[pl.ds(c * PULL, PULL)], yp_s.at[0], yp_r.at[c], across)
        for c in range(N_PULL)
    ]
    zp_cp = [
        remote(z_out.at[pl.ds(r, m)], z_in.at[pl.ds(r, m)], zp_s.at[0], zp_r.at[k], before)
        for k, (r, m) in enumerate(CHUNKS)
    ]
    dp_cp = [
        remote(dp_out.at[pl.ds(r, m)], dp_in.at[pl.ds(r, m)], dp_s.at[0], dp_r.at[k], sibling)
        for k, (r, m) in enumerate(CHUNKS)
    ]
    dt_cp = remote(dt_out, dt_in, dt_s.at[0], dt_r.at[0], sibling)

    def image_pull(i, m):
        return jnp.dot(W[pl.ds(i, m), :], ST[...], preferred_element_type=jnp.float32)

    def text_pull(j, n):
        return lax.dot_general(W[:, pl.ds(j, n)], SI[...], TN, preferred_element_type=jnp.float32)

    def across_pull(c, n):
        y_out[pl.ds(c * PULL, n * PULL)] = image_pull(ROWS + c * PULL, n * PULL).astype(jnp.bfloat16)
        for i in range(c, c + n):
            yp_cp[i].start()

    def early_across(j):
        gi_ref[pl.ds(0, FIRST)] = jnp.dot(
            W[pl.ds(ROWS, FIRST), pl.ds(0, j)], ST[pl.ds(0, j)], preferred_element_type=jnp.float32
        )

    def late_across(j):
        rest = jnp.dot(
            W[pl.ds(ROWS, FIRST), pl.ds(j, 4 * ROWS - j)], ST[pl.ds(j, 4 * ROWS - j)],
            preferred_element_type=jnp.float32,
        )
        y_out[pl.ds(0, FIRST)] = (gi_ref[pl.ds(0, FIRST)] + rest).astype(jnp.bfloat16)
        for i in range(FIRST // PULL):
            yp_cp[i].start()

    def first_text(i, m):
        m0 = CHUNKS[0][1]
        return lax.dot_general(
            W[pl.ds(i, m), pl.ds(OWN_TEXT, 2 * m0)], SI[pl.ds(i, m)], TN, preferred_element_type=jnp.float32
        )

    def prev_leave(pull, first, last):
        r = CHUNKS[first][0]
        for k in range(first, last):
            at, m = CHUNKS[k]
            mine = 2 * (at - r)
            prev_own[pl.ds(at, m)] = pull[mine:mine + m]
            dp_out[pl.ds(at, m)] = pull[mine + m:mine + 2 * m].astype(jnp.bfloat16)
            dp_cp[k].start()

    def prev_pull(first, last):
        r, rows = CHUNKS[first][0], sum(m for _, m in CHUNKS[first:last])
        prev_leave(text_pull(OWN_TEXT + 2 * r, 2 * rows), first, last)

    def prev_send(k):
        r, m = CHUNKS[k]
        rows = pl.ds(r, m)
        dp_cp[k].wait_recv()
        z_out[rows] = (prev_own[rows] + dp_in[rows].astype(jnp.float32)).astype(jnp.bfloat16)
        zp_cp[k].start()

    @pl.when(place != 0)
    def _():
        pass_on(1, 0, 1)
        last = N_CH - 1
        for k in range(last):
            step(k)
        r, m = CHUNKS[last]
        j = OWN_TEXT + 2 * r
        early = pl.ds(0, 2 * CHUNKS[0][1])
        gt_ref[early] = first_text(0, ROWS + r)
        early_across(j)
        step(last)
        second = OWN_TEXT + 2 * CHUNKS[1][0]
        study(ROWS + r, m, OWN_TEXT, second - OWN_TEXT)
        prev_leave(gt_ref[early] + first_text(ROWS + r, m), 0, 1)
        study(ROWS + r, m, second, j - second)
        prev_pull(1, 2)
        f_cp[last][1].wait_recv()
        study(ROWS, FIRST, j, 2 * m)
        late_across(j)
        prev_send(0)
        study(ROWS + r, m, 0, OWN_TEXT)
        study(0, ROWS, j, 2 * m)
        study(ROWS + FIRST, ROWS - FIRST, j, 2 * m)

    @pl.when(place == 0)
    def _():
        last = N_CH - 1
        r, m = CHUNKS[last]
        mid = CHUNKS[SPLIT][0]
        j = OWN_TEXT + 2 * mid
        for k in range(last):
            for half, tile in ((0, teach), (1, study)):
                y_cp[k][half].wait_recv()
                tile(ROWS + CHUNKS[k][0], CHUNKS[k][1], 0, OWN_TEXT)
            if k == 1:
                arrive(0, 0)
                arrive(0, 1)
        for k in (*range(1, SPLIT), *FAR[:-1]):
            arrive(k, 0)
            arrive(k, 1)
        for half, tile in ((0, teach), (1, study)):
            for k in range(SPLIT):
                f_cp[k][half].wait_recv()
            tile(0, ROWS + r, OWN_TEXT, j - OWN_TEXT)
        early_across(j)
        width = 2 * (ROWS - mid)
        for half, tile in ((0, teach), (1, study)):
            for k in (*range(SPLIT, FAR[0]), last):
                arrive(k, half)
            y_cp[last][half].wait_recv()
            tile(ROWS + r, m, 0, j)
            if half == 1:
                prev_pull(0, 1)
                prev_pull(1, 2)
            for k in range(SPLIT, N_CH):
                f_cp[k][half].wait_recv()
            if half == 0:
                tile(0, 2 * ROWS, j, width)
        study(ROWS, FIRST, j, width)
        late_across(j)
        prev_send(0)
        study(0, ROWS, j, width)
        study(ROWS + FIRST, ROWS - FIRST, j, width)

    across_pull(2, 4)
    prev_send(1)
    prev_pull(2, N_CH)
    for k in range(2, N_CH):
        prev_send(k)
    dt_out[...] = text_pull(ROWS, ROWS).astype(jnp.bfloat16)
    dt_cp.start()
    img_own[...] = image_pull(0, ROWS)
    txt_own[...] = text_pull(0, ROWS)
    dt_cp.wait_recv()

    def project(pull, raw, inverse, scale):
        row = raw.astype(jnp.float32) * inverse
        grown = scale * pull
        return (grown - row * jnp.sum(row * grown, axis=-1, keepdims=True)) * inverse

    def finish_image(c):
        rows = pl.ds(c * PULL, PULL)
        yp_cp[c].wait_recv()
        pull = img_own[rows] + y_in[rows].astype(jnp.float32)
        gi_ref[rows] = project(pull, raw_si[rows], inv_i[rows], s_scale)

    def finish_text(k):
        r, m = CHUNKS[k]
        rows = pl.ds(r, m)
        zp_cp[k].wait_recv()
        pull = txt_own[rows] + dt_in[rows].astype(jnp.float32) + z_in[rows].astype(jnp.float32)
        gt_ref[rows] = project(pull, raw_st[rows], inv_t[rows], s_scale)

    for image, text in ((0, 0), (1, None), (2, 1), (3, 2), (4, 3), (5, 4)):
        finish_image(image)
        if text is not None:
            finish_text(text)

    near = CHUNKS[FAR[0]][0]
    sent = [
        (y_out, yp_s.at[0]), (z_out, zp_s.at[0]), (dp_out, dp_s.at[0]), (dt_out, dt_s.at[0]),
    ]
    for half, (image, text) in enumerate(((TI, TT), (SI, ST))):
        whole = pl.ds(0, ROWS)
        sent += [(image.at[whole], y_s.at[half]), (text.at[whole], d_s.at[half]), (text.at[whole], f_s.at[half])]
        sent += [(text.at[pl.ds(0, near)], z_s.at[half])]
    for src, sem in sent:
        remote(src, src, sem, sem, sibling).wait_send()

    @pl.when(relays)
    def _():
        for half, stay in enumerate((far_t, far_s)):
            remote(stay, stay, q_s.at[half], q_s.at[half], sibling).wait_send()

    @pl.when(place != RUN - 1)
    def _():
        for half, text in enumerate((TT, ST)):
            rows = text.at[pl.ds(near, ROWS - near)]
            remote(rows, rows, z_s.at[2 + half], z_s.at[2 + half], sibling).wait_send()


def write_kernel(gi_ref, gt_ref, gi_hbm, gt_hbm, sem):
    copies = []
    for k in range(N_WRITE):
        rows = pl.ds(k * (ROWS // N_WRITE), ROWS // N_WRITE)
        for n, (src, dst) in enumerate(((gi_ref, gi_hbm), (gt_ref, gt_hbm))):
            copies.append(pltpu.make_async_copy(src.at[rows], dst.at[rows], sem.at[k, n]))
    for copy in copies:
        copy.start()
    for copy in copies:
        copy.wait()


def per_device(si, st, ti, tt, ss, sb, ts, tb):
    half, full = jnp.bfloat16, jnp.float32
    dma = pltpu.SemaphoreType.DMA
    smem = pl.BlockSpec(memory_space=pltpu.SMEM)
    hbm = pl.BlockSpec(memory_space=pltpu.HBM)
    free = pl.BlockSpec(memory_space=pl.ANY)
    part = lambda dtype: pltpu.VMEM((ROWS, D_S), dtype)
    grads = pl.pallas_call(
        kernel,
        out_shape=(jax.ShapeDtypeStruct((ROWS, D_S), full),) * 2,
        in_specs=[smem] * 4 + [hbm] * 4,
        out_specs=(pl.BlockSpec(memory_space=pltpu.VMEM),) * 2,
        scratch_shapes=[
            part(half), part(half), pltpu.VMEM((ROWS, D_T), half), pltpu.VMEM((ROWS, D_T), half),
            pltpu.VMEM((ROWS, 1), full), pltpu.VMEM((ROWS, 1), full),
            pltpu.VMEM((2 * ROWS, D_S), half), pltpu.VMEM((2 * ROWS, D_T), half),
            pltpu.VMEM((4 * ROWS, D_S), half), pltpu.VMEM((4 * ROWS, D_T), half),
            pltpu.VMEM((2 * ROWS, 4 * ROWS), full), pltpu.VMEM((2 * ROWS, 4 * ROWS), half),
            part(full), part(full), part(full),
            *[part(half)] * 8,
            pltpu.VMEM((FAR_ROWS, D_T), half), pltpu.VMEM((FAR_ROWS, D_S), half),
            pltpu.SemaphoreType.REGULAR, dma((2, 4)),
            dma((2,)), dma((2 * len(FAR),)),
            dma((2,)), dma((2 * N_CH,)), dma((4,)), dma((2 * N_CH,)), dma((2,)), dma((2,)), dma((2,)), dma((2 * N_CH,)),
            dma((1,)), dma((N_PULL,)), dma((1,)), dma((1,)), dma((1,)), dma((N_CH,)), dma((1,)), dma((N_CH,)),
        ],
        compiler_params=pltpu.CompilerParams(
            collective_id=0, has_side_effects=True, vmem_limit_bytes=44 * 2**20,
        ),
    )(ss, sb, ts, tb, *[pltpu.with_memory_space_constraint(x, pltpu.HBM) for x in (si, st, ti, tt)])
    return pl.pallas_call(
        write_kernel,
        out_shape=(jax.ShapeDtypeStruct((ROWS, D_S), full),) * 2,
        in_specs=[free, free],
        out_specs=(hbm, hbm),
        scratch_shapes=[dma((N_WRITE, 2))],
        compiler_params=pltpu.CompilerParams(vmem_limit_bytes=2**20),
    )(*grads)


def solution(mesh):
    row = P(("loop", "grp"), None)
    return jax.shard_map(
        per_device,
        mesh=mesh,
        in_specs=(row, row, row, row, P(), P(), P(), P()),
        out_specs=(row, row),
        check_vma=False,
    )
```

```python
import functools

import jax
import jax.numpy as jnp
from jax import lax
from jax.experimental import pallas as pl
from jax.experimental.pallas import tpu as pltpu
from jax.sharding import PartitionSpec as P

MESH = pl.DeviceIdType.MESH
N_LOOP = 64
HOP = 3
RUN = 2 * HOP + 2
ROWS = 384
D_S = 768
D_T = 1152
CHUNKS = ((0, 64), (64, 128), (192, 64), (256, 64), (320, 64))
N_CH = len(CHUNKS)
FAR = (3, 4)
FAR_ROWS = 128
SPLIT = 2
RELAY = ((1, 1, 1, 4), (1, 2, 0, 1), (2, 2, 1, 2), (3, 2, 2, 4))
N_WRITE = 2
PULL = 64
FIRST = 2 * PULL
PIECES = ((0, FIRST), *((r, PULL) for r in range(FIRST, ROWS, PULL)))
OWN_TEXT = 2 * ROWS

NT = (((1,), (1,)), ((), ()))
TN = (((0,), (0,)), ((), ()))


def partners():
    loop = lax.axis_index("loop")
    grp = lax.axis_index("grp")
    chip = grp // 2
    core = grp % 2
    place = loop % RUN
    swapped = (1 - chip) * 2 + core

    def at(step, swap):
        side = jnp.where(swap, swapped, grp)
        return ((loop + step + N_LOOP) % N_LOOP, side)

    across = (loop, swapped)
    sibling = (loop, chip * 2 + 1 - core)
    after = at(1, place == RUN - 1)
    before = at(-1, place == 0)
    return core, place, across, sibling, after, before, at


def kernel(
    ss_ref, sb_ref, ts_ref, tb_ref, si_hbm, st_hbm, ti_hbm, tt_hbm, gi_ref, gt_ref,
    raw_si, raw_st, raw_ti, raw_tt, inv_i, inv_t,
    SI, TI, ST, TT, TG, W,
    img_own, txt_own, prev_own,
    y_out, y_in, dt_out, dt_in, dp_out, dp_in, z_out, z_in,
    far_t, far_s,
    gate, in_sem,
    q_s, q_r,
    y_s, y_r, z_s, z_r, d_s, d_r, f_s, f_r,
    yp_s, yp_r, dt_s, dt_r, dp_s, dp_r, zp_s, zp_r,
):
    core, place, across, sibling, after, before, at = partners()
    s_scale, s_bias, t_scale, t_bias = ss_ref[0], sb_ref[0], ts_ref[0], tb_ref[0]

    def remote(src, dst, ssem, rsem, dev):
        return pltpu.make_async_remote_copy(
            src_ref=src, dst_ref=dst, send_sem=ssem, recv_sem=rsem,
            device_id=dev, device_id_type=MESH,
        )

    loads = [
        [
            pltpu.make_async_copy(src.at[pl.ds(r, m)], dst.at[pl.ds(r, m)], in_sem.at[k, n])
            for n, (src, dst) in enumerate(
                ((ti_hbm, raw_ti), (tt_hbm, raw_tt), (si_hbm, raw_si), (st_hbm, raw_st))
            )
        ]
        for k, (r, m) in enumerate((CHUNKS[0], (CHUNKS[1][0], ROWS - CHUNKS[1][0])))
    ]
    for group in loads:
        for copy in group:
            copy.start()
    barrier = pltpu.get_barrier_semaphore()
    relays = place % HOP == 1

    def report(dev, to):
        pl.semaphore_signal(barrier, inc=1, device_id=(dev[0], dev[1] // 2 * 2 + to), device_id_type=MESH)

    report(across, 0)
    report(before, 1)

    @pl.when(core == 1)
    def _():
        report(sibling, 0)

    @pl.when(place == 1 + HOP)
    def _():
        report(at(HOP, False), 1)

    @pl.when(place == 1)
    def _():
        report(at(HOP - RUN, True), 1)

    @pl.when(place == 0)
    def _():
        report(at(1, False), 1)

    def wait_gate(counter, amount):
        @pl.when(core == counter)
        def _():
            pl.semaphore_wait(barrier, amount)
            pl.semaphore_signal(gate, inc=1, device_id=sibling, device_id_type=MESH)

        @pl.when(core != counter)
        def _():
            pl.semaphore_wait(gate, 1)

    def unit(raw, rows, out, at, keep=None):
        wide = raw[rows].astype(jnp.float32)
        inverse = lax.rsqrt(jnp.sum(wide * wide, axis=-1, keepdims=True) + 1e-06)
        out[at] = (wide * inverse).astype(jnp.bfloat16)
        if keep is not None:
            keep[rows] = inverse

    def prev_at(k):
        r, m = CHUNKS[k]
        return pl.ds(OWN_TEXT + 2 * r, m), pl.ds(OWN_TEXT + 2 * r + m, m)

    y_cp, z_cp, d_cp, f_cp, far_cp = [], [], [], [], []
    for k, (r, m) in enumerate(CHUNKS):
        own = pl.ds(r, m)
        po, ps = prev_at(k)
        y_cp.append((
            remote(TI.at[own], TI.at[pl.ds(ROWS + r, m)], y_s.at[0], y_r.at[2 * k], across),
            remote(SI.at[own], SI.at[pl.ds(ROWS + r, m)], y_s.at[1], y_r.at[2 * k + 1], across),
        ))
        z_cp.append((
            remote(TT.at[own], TT.at[po], z_s.at[2 * (k in FAR)], z_r.at[2 * k], after),
            remote(ST.at[own], ST.at[po], z_s.at[2 * (k in FAR) + 1], z_r.at[2 * k + 1], after),
        ))
        d_cp.append((
            remote(TT.at[own], TT.at[pl.ds(ROWS + r, m)], d_s.at[0], d_r.at[0], sibling),
            remote(ST.at[own], ST.at[pl.ds(ROWS + r, m)], d_s.at[1], d_r.at[1], sibling),
        ))
        f_cp.append((
            remote(TT.at[po], TT.at[ps], f_s.at[0], f_r.at[2 * k], sibling),
            remote(ST.at[po], ST.at[ps], f_s.at[1], f_r.at[2 * k + 1], sibling),
        ))
        if k in FAR:
            down, over, home = at(-HOP, False), at(RUN - HOP, True), at(-1, False)
            stop = pl.ds(r - CHUNKS[FAR[0]][0], m)
            pairs = []
            for half, (text, stay) in enumerate(((TT, far_t), (ST, far_s))):
                n = 2 * (k - FAR[0]) + half
                pairs.append((
                    remote(text.at[own], stay.at[stop], q_s.at[half], q_r.at[n], down),
                    remote(stay.at[stop], stay.at[stop], q_s.at[half], q_r.at[n], over),
                    remote(stay.at[stop], text.at[po], q_s.at[half], z_r.at[2 * k + half], home),
                ))
            far_cp.extend(pairs)

    def pass_on(hop, first, last):
        @pl.when(place == 1 + HOP * (2 - hop))
        def _():
            for n in range(first, last):
                far_cp[n][0].wait_recv()
                far_cp[n][hop].start()

    def prepare_images(k):
        own = pl.ds(*CHUNKS[k])
        unit(raw_ti, own, TI, own)
        y_cp[k][0].start()
        unit(raw_si, own, SI, own, inv_i)
        y_cp[k][1].start()

    def prepare_text(k):
        own = pl.ds(*CHUNKS[k])
        unit(raw_tt, own, TT, own)
        unit(raw_st, own, ST, own, inv_t)

    for copy in loads[0]:
        copy.wait()
    own = pl.ds(*CHUNKS[0])
    unit(raw_ti, own, TI, own)
    unit(raw_si, own, SI, own, inv_i)
    wait_gate(0, 3)
    for half in (0, 1):
        y_cp[0][half].start()
    unit(raw_tt, own, TT, own)
    unit(raw_st, own, ST, own, inv_t)
    for half in (0, 1):
        d_cp[0][half].start()
    for copy in loads[1]:
        copy.wait()
    wait_gate(1, jnp.where(relays, 4, 2))
    for half in (0, 1):
        z_cp[0][half].start()
    for k in FAR:
        own = pl.ds(*CHUNKS[k])
        for half, norm in ((0, (raw_tt, own, TT, own)), (1, (raw_st, own, ST, own, inv_t))):
            unit(*norm)

            @pl.when(place == RUN - 1)
            def _():
                far_cp[2 * (k - FAR[0]) + half][0].start()
    for k in range(1, N_CH):
        if k not in FAR:
            prepare_text(k)
            for half in (0, 1):
                z_cp[k][half].start()
        for half in (0, 1):
            d_cp[k][half].start()

    @pl.when(place != RUN - 1)
    def _():
        for k in FAR:
            for half in (0, 1):
                z_cp[k][half].start()

    for k in range(1, N_CH):
        prepare_images(k)

    def teach(i, m, j, n):
        dot = lax.dot_general(TI[pl.ds(i, m)], TT[pl.ds(j, n)], NT, preferred_element_type=jnp.float32)
        TG[pl.ds(i, m), pl.ds(j, n)] = jax.nn.sigmoid(t_scale * dot + t_bias)

    def study(i, m, j, n):
        dot = lax.dot_general(SI[pl.ds(i, m)], ST[pl.ds(j, n)], NT, preferred_element_type=jnp.float32)
        at = (pl.ds(i, m), pl.ds(j, n))
        W[at] = (jax.nn.sigmoid(s_scale * dot + s_bias) - TG[at]).astype(jnp.bfloat16)

    teach(0, ROWS, 0, ROWS)
    study(0, ROWS, 0, ROWS)
    for half, text in enumerate((TT, ST)):
        theirs = text.at[pl.ds(ROWS, ROWS)]
        remote(theirs, theirs, d_s.at[half], d_r.at[half], sibling).wait_recv()
    teach(0, ROWS, ROWS, ROWS)
    study(0, ROWS, ROWS, ROWS)

    def arrive(k, half):
        z_cp[k][half].wait_recv()
        f_cp[k][half].start()

    def step(k):
        r, m = CHUNKS[k]
        j = OWN_TEXT + 2 * r
        for half, tile in ((0, teach), (1, study)):
            arrive(k, half)
            y_cp[k][half].wait_recv()
            if k == N_CH - 1 and half == 1:
                break
            tile(ROWS + r, m, 0, j)
            f_cp[k][half].wait_recv()
            tile(0, ROWS + r + m, j, 2 * m)
        for when, hop, first, last in RELAY:
            if when == k + 1:
                pass_on(hop, first, last)

    yp_cp = [
        remote(y_out.at[pl.ds(r, m)], y_in.at[pl.ds(r, m)], yp_s.at[0], yp_r.at[c], across)
        for c, (r, m) in enumerate(PIECES)
    ]
    zp_cp = [
        remote(z_out.at[pl.ds(r, m)], z_in.at[pl.ds(r, m)], zp_s.at[0], zp_r.at[k], before)
        for k, (r, m) in enumerate(CHUNKS)
    ]
    dp_cp = [
        remote(dp_out.at[pl.ds(r, m)], dp_in.at[pl.ds(r, m)], dp_s.at[0], dp_r.at[k], sibling)
        for k, (r, m) in enumerate((*CHUNKS[:2], (CHUNKS[2][0], ROWS - CHUNKS[2][0])))
    ]
    dt_cp = remote(dt_out, dt_in, dt_s.at[0], dt_r.at[0], sibling)

    def image_pull(i, m):
        return jnp.dot(W[pl.ds(i, m), :], ST[...], preferred_element_type=jnp.float32)

    def text_pull(j, n):
        return lax.dot_general(W[:, pl.ds(j, n)], SI[...], TN, preferred_element_type=jnp.float32)

    def across_rest():
        rest = ROWS - FIRST
        y_out[pl.ds(FIRST, rest)] = image_pull(ROWS + FIRST, rest).astype(jnp.bfloat16)
        for copy in yp_cp[1:]:
            copy.start()

    def early_across(j):
        gi_ref[pl.ds(0, FIRST)] = jnp.dot(
            W[pl.ds(ROWS, FIRST), pl.ds(0, j)], ST[pl.ds(0, j)], preferred_element_type=jnp.float32
        )

    def late_across(j):
        rest = jnp.dot(
            W[pl.ds(ROWS, FIRST), pl.ds(j, 4 * ROWS - j)], ST[pl.ds(j, 4 * ROWS - j)],
            preferred_element_type=jnp.float32,
        )
        y_out[pl.ds(0, FIRST)] = (gi_ref[pl.ds(0, FIRST)] + rest).astype(jnp.bfloat16)
        yp_cp[0].start()

    def first_text(i, m):
        m0 = CHUNKS[0][1]
        return lax.dot_general(
            W[pl.ds(i, m), pl.ds(OWN_TEXT, 2 * m0)], SI[pl.ds(i, m)], TN, preferred_element_type=jnp.float32
        )

    def prev_leave(pull, first, last):
        r = CHUNKS[first][0]
        for k in range(first, last):
            at, m = CHUNKS[k]
            mine = 2 * (at - r)
            prev_own[pl.ds(at, m)] = pull[mine:mine + m]
            dp_out[pl.ds(at, m)] = pull[mine + m:mine + 2 * m].astype(jnp.bfloat16)
        dp_cp[first].start()

    def prev_pull(first, last):
        r, rows = CHUNKS[first][0], sum(m for _, m in CHUNKS[first:last])
        prev_leave(text_pull(OWN_TEXT + 2 * r, 2 * rows), first, last)

    def prev_send(k):
        r, m = CHUNKS[k]
        rows = pl.ds(r, m)
        if k < len(dp_cp):
            dp_cp[k].wait_recv()
        z_out[rows] = (prev_own[rows] + dp_in[rows].astype(jnp.float32)).astype(jnp.bfloat16)
        zp_cp[k].start()

    @pl.when(place != 0)
    def _():
        pass_on(1, 0, 1)
        last = N_CH - 1
        for k in range(last):
            step(k)
        r, m = CHUNKS[last]
        j = OWN_TEXT + 2 * r
        early = pl.ds(0, 2 * CHUNKS[0][1])
        gt_ref[early] = first_text(0, ROWS + r)
        early_across(j)
        step(last)
        second = OWN_TEXT + 2 * CHUNKS[1][0]
        study(ROWS + r, m, OWN_TEXT, second - OWN_TEXT)
        prev_leave(gt_ref[early] + first_text(ROWS + r, m), 0, 1)
        study(ROWS + r, m, second, j - second)
        prev_pull(1, 2)
        f_cp[last][1].wait_recv()
        study(ROWS, FIRST, j, 2 * m)
        late_across(j)
        prev_send(0)
        study(ROWS + r, m, 0, OWN_TEXT)
        study(0, ROWS, j, 2 * m)
        study(ROWS + FIRST, ROWS - FIRST, j, 2 * m)

    @pl.when(place == 0)
    def _():
        last = N_CH - 1
        r, m = CHUNKS[last]
        mid = CHUNKS[SPLIT][0]
        j = OWN_TEXT + 2 * mid
        for k in range(last):
            for half, tile in ((0, teach), (1, study)):
                y_cp[k][half].wait_recv()
                tile(ROWS + CHUNKS[k][0], CHUNKS[k][1], 0, OWN_TEXT)
            if k == 1:
                arrive(0, 0)
                arrive(0, 1)
        for k in (*range(1, SPLIT), *FAR[:-1]):
            arrive(k, 0)
            arrive(k, 1)
        for half, tile in ((0, teach), (1, study)):
            for k in range(SPLIT):
                f_cp[k][half].wait_recv()
            tile(0, ROWS + r, OWN_TEXT, j - OWN_TEXT)
        early_across(j)
        width = 2 * (ROWS - mid)
        for half, tile in ((0, teach), (1, study)):
            for k in (*range(SPLIT, FAR[0]), last):
                arrive(k, half)
            y_cp[last][half].wait_recv()
            tile(ROWS + r, m, 0, j)
            if half == 1:
                prev_pull(0, 1)
                prev_pull(1, 2)
            for k in range(SPLIT, N_CH):
                f_cp[k][half].wait_recv()
            if half == 0:
                tile(0, 2 * ROWS, j, width)
        study(ROWS, FIRST, j, width)
        late_across(j)
        prev_send(0)
        study(0, ROWS, j, width)
        study(ROWS + FIRST, ROWS - FIRST, j, width)

    across_rest()
    prev_send(1)
    prev_pull(2, N_CH)
    for k in range(2, N_CH):
        prev_send(k)
    dt_out[...] = text_pull(ROWS, ROWS).astype(jnp.bfloat16)
    dt_cp.start()
    img_own[...] = image_pull(0, ROWS)
    txt_own[...] = text_pull(0, ROWS)
    dt_cp.wait_recv()

    def project(pull, raw, inverse, scale):
        row = raw.astype(jnp.float32) * inverse
        grown = scale * pull
        return (grown - row * jnp.sum(row * grown, axis=-1, keepdims=True)) * inverse

    def finish_image(c):
        rows = pl.ds(*PIECES[c])
        yp_cp[c].wait_recv()
        pull = img_own[rows] + y_in[rows].astype(jnp.float32)
        gi_ref[rows] = project(pull, raw_si[rows], inv_i[rows], s_scale)

    def finish_text(k):
        r, m = CHUNKS[k]
        rows = pl.ds(r, m)
        zp_cp[k].wait_recv()
        pull = txt_own[rows] + dt_in[rows].astype(jnp.float32) + z_in[rows].astype(jnp.float32)
        gt_ref[rows] = project(pull, raw_st[rows], inv_t[rows], s_scale)

    for image, text in ((None, 0), (0, None), (1, 1), (2, None), (3, 2), (None, 3), (4, 4)):
        if image is not None:
            finish_image(image)
        if text is not None:
            finish_text(text)

    near = CHUNKS[FAR[0]][0]
    sent = [
        (y_out, yp_s.at[0]), (z_out, zp_s.at[0]), (dp_out, dp_s.at[0]), (dt_out, dt_s.at[0]),
    ]
    for half, (image, text) in enumerate(((TI, TT), (SI, ST))):
        whole = pl.ds(0, ROWS)
        sent += [(image.at[whole], y_s.at[half]), (text.at[whole], d_s.at[half]), (text.at[whole], f_s.at[half])]
        sent += [(text.at[pl.ds(0, near)], z_s.at[half])]
    for src, sem in sent:
        remote(src, src, sem, sem, sibling).wait_send()

    @pl.when(relays)
    def _():
        for half, stay in enumerate((far_t, far_s)):
            remote(stay, stay, q_s.at[half], q_s.at[half], sibling).wait_send()

    @pl.when(place != RUN - 1)
    def _():
        for half, text in enumerate((TT, ST)):
            rows = text.at[pl.ds(near, ROWS - near)]
            remote(rows, rows, z_s.at[2 + half], z_s.at[2 + half], sibling).wait_send()


def write_kernel(gi_ref, gt_ref, gi_hbm, gt_hbm, sem):
    copies = []
    for k in range(N_WRITE):
        rows = pl.ds(k * (ROWS // N_WRITE), ROWS // N_WRITE)
        for n, (src, dst) in enumerate(((gi_ref, gi_hbm), (gt_ref, gt_hbm))):
            copies.append(pltpu.make_async_copy(src.at[rows], dst.at[rows], sem.at[k, n]))
    for copy in copies:
        copy.start()
    for copy in copies:
        copy.wait()


def per_device(si, st, ti, tt, ss, sb, ts, tb):
    half, full = jnp.bfloat16, jnp.float32
    dma = pltpu.SemaphoreType.DMA
    smem = pl.BlockSpec(memory_space=pltpu.SMEM)
    hbm = pl.BlockSpec(memory_space=pltpu.HBM)
    free = pl.BlockSpec(memory_space=pl.ANY)
    part = lambda dtype: pltpu.VMEM((ROWS, D_S), dtype)
    grads = pl.pallas_call(
        kernel,
        out_shape=(jax.ShapeDtypeStruct((ROWS, D_S), full),) * 2,
        in_specs=[smem] * 4 + [hbm] * 4,
        out_specs=(pl.BlockSpec(memory_space=pltpu.VMEM),) * 2,
        scratch_shapes=[
            part(half), part(half), pltpu.VMEM((ROWS, D_T), half), pltpu.VMEM((ROWS, D_T), half),
            pltpu.VMEM((ROWS, 1), full), pltpu.VMEM((ROWS, 1), full),
            pltpu.VMEM((2 * ROWS, D_S), half), pltpu.VMEM((2 * ROWS, D_T), half),
            pltpu.VMEM((4 * ROWS, D_S), half), pltpu.VMEM((4 * ROWS, D_T), half),
            pltpu.VMEM((2 * ROWS, 4 * ROWS), full), pltpu.VMEM((2 * ROWS, 4 * ROWS), half),
            part(full), part(full), part(full),
            *[part(half)] * 8,
            pltpu.VMEM((FAR_ROWS, D_T), half), pltpu.VMEM((FAR_ROWS, D_S), half),
            pltpu.SemaphoreType.REGULAR, dma((2, 4)),
            dma((2,)), dma((2 * len(FAR),)),
            dma((2,)), dma((2 * N_CH,)), dma((4,)), dma((2 * N_CH,)), dma((2,)), dma((2,)), dma((2,)), dma((2 * N_CH,)),
            dma((1,)), dma((len(PIECES),)), dma((1,)), dma((1,)), dma((1,)), dma((3,)), dma((1,)), dma((N_CH,)),
        ],
        compiler_params=pltpu.CompilerParams(
            collective_id=0, has_side_effects=True, vmem_limit_bytes=44 * 2**20,
        ),
    )(ss, sb, ts, tb, *[pltpu.with_memory_space_constraint(x, pltpu.HBM) for x in (si, st, ti, tt)])
    return pl.pallas_call(
        write_kernel,
        out_shape=(jax.ShapeDtypeStruct((ROWS, D_S), full),) * 2,
        in_specs=[free, free],
        out_specs=(hbm, hbm),
        scratch_shapes=[dma((N_WRITE, 2))],
        compiler_params=pltpu.CompilerParams(vmem_limit_bytes=2**20),
    )(*grads)


def solution(mesh):
    row = P(("loop", "grp"), None)
    return jax.shard_map(
        per_device,
        mesh=mesh,
        in_specs=(row, row, row, row, P(), P(), P(), P()),
        out_specs=(row, row),
        check_vma=False,
    )
```
